256 devices in a mesh: req: 32 (over z, x), head: 8 (over y, core).
Axes of the slice: x: 4, y: 4, z: 8, core: 2. Of those that a mesh axis runs over, the one named last changes fastest.
Arguments:
- hidden: bfloat16 [64, 128, 8192], P('req', None, 'head'), may hold values from -6 to 6
- w_query: bfloat16 [8192, 8192], P('req', 'head'), may hold values from -0.0625 to 0.0625
- w_key: bfloat16 [8192, 1024], P('req', 'head'), may hold values from -0.0625 to 0.0625
- w_value: bfloat16 [8192, 1024], P('req', 'head'), may hold values from -0.0625 to 0.0625
- doc_keys: bfloat16 [512, 8, 128, 128], P('req', 'head'), may hold values from -320 to 320
- doc_values: bfloat16 [512, 8, 128, 128], P('req', 'head'), may hold values from -8 to 8
- slot_counts: int32 [512, 8], P(None, 'head'), may hold values from 1 to 8
- kept_blocks: int32 [512, 8, 8], P(None, 'head'), may hold values from 0 to 15, as said below
- doc_ids: int32 [64, 16], replicated, may hold values from 0 to 511, as said below
- doc_place: int32 [512], replicated, may hold values from 0 to 511, as said below
- recompute_rows: int32 [64, 128], P('req'), may hold values from 0 to 4095, as said below
Outputs:
- attended: bfloat16 [64, 128, 8192], P('req', None, 'head')
- new_keys: bfloat16 [64, 128, 1024], P('req', None, 'head')
- new_values: bfloat16 [64, 128, 1024], P('req', None, 'head')
The draws below stay inside these ranges and needn't reach their ends.
Inputs may be any that keep to these rules, and one draw needn't show every extreme that they name: `doc_ids`: among the 32 document slots of the requests of one index of req, at most 2 name documents whose doc_place lies in one owner's 16 rows, counting repeats; in every such block some owner has exactly 2. `doc_place`: a permutation; document d sits on owner doc_place[d] // 16. `kept_blocks`: for each document and head the 8 entries are distinct and rising. `recompute_rows`: distinct and rising within a request.
All inputs are finite; a program needn't handle non-finite values.
Results may differ from the reference program's by a relative error of at most 0.0085.
The reference program's roundings to bfloat16 on the way (of `queries` and `probs`) count: a program that leaves them out, or rounds other values in their place, can miss the bound.
Values may be sent and summed in bfloat16 or wider, within the bound.
A program may use at most 128 MiB of HBM per device.

```python
import math
import jax
import jax.numpy as jnp
from jax import lax

D = 8192
QH = 64
KVH = 8
HD = 128
BLK = 16
DOC_BLKS = 16
SLOTS = 8
NDOC = 16
RECOMP = 128
REQ_DEV = 2
DOC_DEV = 16
REQS = 64
DOCS = 512
CTX = 4096


def layout(key):
    owners = DOCS // DOC_DEV
    refs = REQ_DEV * NDOC
    place = jax.random.permutation(jax.random.fold_in(key, 101), DOCS).astype(jnp.int32)
    inverse = jnp.argsort(place).astype(jnp.int32)
    share = refs // owners
    base = jnp.tile(jnp.arange(owners, dtype=jnp.int32), share)

    def one_block(block_key):
        first, second, third, fourth = jax.random.split(block_key, 4)
        heavy = jax.random.randint(first, (), 0, owners)
        emptied = (heavy + jax.random.randint(second, (), 1, owners)) % owners
        chosen = jnp.where(base == emptied, heavy, base).astype(jnp.int32)
        chosen = jax.random.permutation(third, chosen)
        local = jax.random.randint(fourth, (refs,), 0, DOC_DEV).astype(jnp.int32)
        return inverse[chosen * DOC_DEV + local]
    blocks = jax.vmap(one_block)(jax.random.split(jax.random.fold_in(key, 102), owners))
    return (place, blocks.reshape(REQS, NDOC).astype(jnp.int32))


def draw_doc_place(key, part):
    return layout(key)[0]


def draw_doc_ids(key, part):
    return layout(key)[1]


def draw_kept_blocks(key, part):
    key = jax.random.fold_in(key, 3)
    keys = jax.random.split(key, DOCS * KVH)
    rows = jax.vmap(lambda one_key: jnp.sort(jax.random.permutation(one_key, DOC_BLKS)[:SLOTS]))(keys)
    return rows.reshape(DOCS, KVH, SLOTS).astype(jnp.int32)


def draw_recompute_rows(key, part):
    key = jax.random.fold_in(key, 4)
    keys = jax.random.split(key, REQS)
    rows = jax.vmap(lambda one_key: jnp.sort(jax.random.permutation(one_key, CTX)[:RECOMP]))(keys)
    return rows.astype(jnp.int32)


def draw_doc_keys(key, part):
    key = jax.random.fold_in(key, 5)
    first = jax.random.fold_in(key, 0)
    values = jnp.clip(jax.random.normal(first, (DOCS, KVH, SLOTS * BLK, HD), jnp.float32), -4.0, 4.0) * 2.0
    return values.astype(jnp.bfloat16)


def place_ends(entries, own_key, smallest, largest):
    dims = entries.shape
    spot = [jax.random.randint(jax.random.fold_in(own_key, axis), (), 0, dims[axis]) for axis in range(len(dims))]
    entries = entries.at[tuple(spot)].set(smallest)
    longest = dims.index(max(dims))
    spot[longest] = (spot[longest] + 1) % dims[longest]
    return entries.at[tuple(spot)].set(largest)


def levels(stream_key, shape, shards, low, top_value):
    gain, own = 1.0, jax.random.fold_in(stream_key, 6)
    for axis_at, blocks in shards:
        heights = jnp.exp(jax.random.uniform(jax.random.fold_in(own, axis_at), (blocks,), jnp.float32, low / len(shards), top_value / len(shards)))
        gain = gain * jnp.repeat(heights, shape[axis_at] // blocks).reshape([-1 if axis == axis_at else 1 for axis in range(len(shape))])
    return gain


def normal_values(stream_key, extent, width, most, shards=(), kind=jnp.bfloat16):
    values = width * jax.random.normal(stream_key, extent, jnp.float32)
    if shards:
        values = values * levels(stream_key, extent, shards, -0.22, 0.18)
    return jnp.clip(values, -most, most).astype(kind)


def setup_inputs(seed: int = 0) -> dict:
    key_of = jax.random.split(jax.random.key(seed), 12)
    hidden = normal_values(key_of[0], (REQS, RECOMP, D), 1.0, 6.0, ((0, 32), (2, 8)))
    w_query = normal_values(key_of[1], (D, QH * HD), D ** -0.5, 0.0625, ((0, 32), (1, 8)))
    w_key = normal_values(key_of[2], (D, KVH * HD), D ** -0.5, 0.0625, ((0, 32), (1, 8)))
    w_value = normal_values(key_of[3], (D, KVH * HD), D ** -0.5, 0.0625, ((0, 32), (1, 8)))
    doc_keys = draw_doc_keys(jax.random.fold_in(key_of[11], 71), 0)
    doc_values = normal_values(key_of[5], (DOCS, KVH, SLOTS * BLK, HD), 2.0, 8.0, ((0, 32), (1, 8)))
    slot_counts = place_ends(jax.random.randint(key_of[6], (DOCS, KVH), 1, SLOTS + 1), jax.random.fold_in(key_of[6], 1), 1, SLOTS).astype(jnp.int32)
    kept_blocks = draw_kept_blocks(jax.random.fold_in(key_of[11], 71), 0)
    doc_ids = draw_doc_ids(jax.random.fold_in(key_of[11], 71), 0)
    doc_place = draw_doc_place(jax.random.fold_in(key_of[11], 71), 0)
    recompute_rows = draw_recompute_rows(jax.random.fold_in(key_of[11], 71), 0)
    return dict(hidden=hidden, w_query=w_query, w_key=w_key, w_value=w_value, doc_keys=doc_keys, doc_values=doc_values, slot_counts=slot_counts, kept_blocks=kept_blocks, doc_ids=doc_ids, doc_place=doc_place, recompute_rows=recompute_rows)


def reference(hidden, w_query, w_key, w_value, doc_keys, doc_values, slot_counts, kept_blocks, doc_ids, doc_place, recompute_rows):
    group = QH // KVH
    span = SLOTS * BLK
    scale = 1.0 / math.sqrt(HD)

    def one_request(index):
        rows_in = hidden[index]
        queries = jnp.dot(rows_in, w_query, preferred_element_type=jnp.float32).astype(jnp.bfloat16)
        keys_new = jnp.dot(rows_in, w_key, preferred_element_type=jnp.float32).astype(jnp.bfloat16)
        values_new = jnp.dot(rows_in, w_value, preferred_element_type=jnp.float32).astype(jnp.bfloat16)
        ids = doc_ids[index]
        rows_at = doc_place[ids]
        stored_keys = doc_keys[rows_at]
        stored_values = doc_values[rows_at]
        positions = recompute_rows[index]
        offsets = jnp.arange(NDOC, dtype=jnp.int32)[:, None, None] * (DOC_BLKS * BLK)
        inner = jnp.arange(BLK, dtype=jnp.int32)[None, None, :]
        slot_index = jnp.arange(SLOTS, dtype=jnp.int32)[None, :, None]
        outputs = []
        for head_idx in range(KVH):
            blocks = kept_blocks[ids, head_idx]
            count_here = slot_counts[ids, head_idx]
            key_pos = (offsets + blocks[:, :, None] * BLK + inner).reshape(-1)
            valid = (slot_index < count_here[:, None, None]) & (inner >= 0)
            replaced = jnp.any(key_pos[:, None] == positions[None, :], axis=1)
            live = jnp.concatenate([valid.reshape(-1) & jnp.logical_not(replaced), jnp.ones((RECOMP,), bool)])
            context_keys = jnp.concatenate([stored_keys[:, head_idx].reshape(NDOC * span, HD), keys_new[:, head_idx * HD:(head_idx + 1) * HD]], axis=0)
            context_values = jnp.concatenate([stored_values[:, head_idx].reshape(NDOC * span, HD), values_new[:, head_idx * HD:(head_idx + 1) * HD]], axis=0)
            head_queries = queries[:, head_idx * group * HD:(head_idx + 1) * group * HD].reshape(RECOMP, group, HD)
            scores = jnp.einsum('rgd,kd->rgk', head_queries.astype(jnp.float32), context_keys.astype(jnp.float32)) * scale
            scores = jnp.where(live[None, None, :], scores, -jnp.inf)
            peak = lax.optimization_barrier(jnp.max(scores, axis=-1, keepdims=True))
            weights = jnp.exp(scores - peak)
            probs = (weights / lax.optimization_barrier(jnp.sum(weights, axis=-1, keepdims=True))).astype(jnp.bfloat16)
            result = jnp.einsum('rgk,kd->rgd', probs.astype(jnp.float32), context_values.astype(jnp.float32))
            outputs.append(result.astype(jnp.bfloat16).reshape(RECOMP, group * HD))
        return (jnp.concatenate(outputs, axis=1), keys_new, values_new)
    attended, new_keys, new_values = lax.map(one_request, jnp.arange(REQS, dtype=jnp.int32))
    return (attended, new_keys, new_values)
```

```python
import math

import jax
import jax.numpy as jnp
from jax import lax
from jax.experimental import pallas as pl
from jax.experimental.pallas import tpu as pltpu
from jax.sharding import PartitionSpec as P

QH = 64
KVH = 8
HD = 128
BLK = 16
DOC_BLKS = 16
SLOTS = 8
NDOC = 16


def attend(block_queries, context_keys, context_values, live, scale):
    scores = (
        jnp.einsum("rgd,kd->rgk", block_queries, context_keys, preferred_element_type=jnp.float32)
        * scale
    )
    scores = jnp.where(live[None, None, :], scores, -jnp.inf)
    peak = jnp.max(scores, axis=-1, keepdims=True)
    weights = jnp.exp(scores - peak)
    probs = (weights / jnp.sum(weights, axis=-1, keepdims=True)).astype(jnp.bfloat16)
    result = jnp.einsum("rgk,kd->rgd", probs, context_values, preferred_element_type=jnp.float32)
    return result.astype(jnp.bfloat16).reshape(block_queries.shape[0], -1)


def general(
    hidden,
    w_query,
    w_key,
    w_value,
    doc_keys,
    doc_values,
    slot_counts,
    kept_blocks,
    doc_ids,
    doc_place,
    recompute_rows,
):
    req_here, rows_req, width_part = hidden.shape
    total = req_here * rows_req
    heads_here = w_key.shape[1] // HD
    group = QH // KVH
    span = SLOTS * BLK
    scale = 1.0 / math.sqrt(HD)
    owners = lax.axis_size("req")
    mine = lax.axis_index("req")
    docs_here = doc_keys.shape[0]
    refs = req_here * NDOC
    capacity = 2 * (refs // owners)
    whole = lax.all_gather(hidden, "head", axis=2, tiled=True).reshape(total, -1)
    pieces = (
        lax.all_gather(w_query, "req", axis=0, tiled=True),
        lax.all_gather(w_key, "req", axis=0, tiled=True),
        lax.all_gather(w_value, "req", axis=0, tiled=True),
    )
    sums = tuple((jnp.dot(whole, piece, preferred_element_type=jnp.float32) for piece in pieces))
    placed = doc_place[doc_ids]
    owner_all = (placed // docs_here).reshape(owners, refs)
    local_all = (placed % docs_here).reshape(owners, refs)
    order = jnp.arange(refs, dtype=jnp.int32)
    earlier = (owner_all[:, :, None] == owner_all[:, None, :]) & (
        order[None, None, :] < order[None, :, None]
    )
    rank = jnp.sum(earlier.astype(jnp.int32), axis=2)
    slot_ids = jnp.arange(capacity, dtype=jnp.int32)
    match = (
        (owner_all == mine)[:, :, None] & (rank[:, :, None] == slot_ids[None, None, :])
    ).astype(jnp.int32)
    picked = jnp.sum(match * local_all[:, :, None], axis=1)
    used = jnp.sum(match, axis=1) > 0

    def pack(cache):
        selected = cache[picked]
        return jnp.where(used[:, :, None, None, None], selected, jnp.zeros_like(selected))

    got_keys = lax.all_to_all(pack(doc_keys), "req", split_axis=0, concat_axis=0, tiled=True)
    got_values = lax.all_to_all(pack(doc_values), "req", split_axis=0, concat_axis=0, tiled=True)
    own_owner = lax.dynamic_index_in_dim(owner_all, mine, 0, False)
    own_rank = lax.dynamic_index_in_dim(rank, mine, 0, False)
    where_row = own_owner * capacity + own_rank
    tail = got_keys.shape[2:]
    fetched_keys = got_keys.reshape((owners * capacity,) + tail)[where_row].reshape(
        (req_here, NDOC) + tail
    )
    fetched_values = got_values.reshape((owners * capacity,) + tail)[where_row].reshape(
        (req_here, NDOC) + tail
    )
    fetched_keys, fetched_values = (fetched_keys, fetched_values)
    queries = sums[0].astype(jnp.bfloat16).reshape(req_here, rows_req, heads_here, group, HD)
    keys_new = sums[1].astype(jnp.bfloat16).reshape(req_here, rows_req, heads_here, HD)
    values_new = sums[2].astype(jnp.bfloat16).reshape(req_here, rows_req, heads_here, HD)
    my_ids = lax.dynamic_slice_in_dim(doc_ids, mine * req_here, req_here, 0)
    offsets = jnp.arange(NDOC, dtype=jnp.int32)[:, None, None] * (DOC_BLKS * BLK)
    inner = jnp.arange(BLK, dtype=jnp.int32)[None, None, :]
    slot_index = jnp.arange(SLOTS, dtype=jnp.int32)[None, :, None]
    block_rows = 128
    request_outputs = []
    for request in range(req_here):
        ids = my_ids[request]
        positions = recompute_rows[request]
        blocks = kept_blocks[ids, 0]
        count_here = slot_counts[ids, 0]
        key_pos = (offsets + blocks[:, :, None] * BLK + inner).reshape(-1)
        valid = (slot_index < count_here[:, None, None]) & (inner >= 0)
        replaced = jnp.any(key_pos[:, None] == positions[None, :], axis=1)
        live = jnp.concatenate(
            [valid.reshape(-1) & jnp.logical_not(replaced), jnp.ones((rows_req,), bool)]
        )
        context_keys = jnp.concatenate(
            [fetched_keys[request, :, 0].reshape(NDOC * span, HD), keys_new[request, :, 0]], axis=0
        )
        context_values = jnp.concatenate(
            [fetched_values[request, :, 0].reshape(NDOC * span, HD), values_new[request, :, 0]],
            axis=0,
        )
        query_blocks = queries[request, :, 0].reshape(rows_req // block_rows, block_rows, group, HD)
        result = lax.map(
            lambda block_queries: attend(block_queries, context_keys, context_values, live, scale),
            query_blocks,
        )
        head_outputs = result.reshape(rows_req, group * HD)
        request_outputs.append(head_outputs)
    attended = jnp.stack(request_outputs, axis=0)
    return (
        attended,
        keys_new.reshape(req_here, rows_req, heads_here * HD),
        values_new.reshape(req_here, rows_req, heads_here * HD),
    )


MESH = pl.DeviceIdType.MESH
NX, NZ, NY = 4, 8, 4
COLS = 256
CHUNKS = 5


def exchange_kernel(
    tab,
    exsel,
    hid,
    dk,
    dv,
    wq,
    wk,
    wv,
    q_out,
    nk_out,
    nv_out,
    docs_out,
    hg,
    wg,
    part,
    r1,
    r2,
    xs,
    xr,
    ex,
    zr,
    own_sem,
    hx_s,
    hx_r,
    hy_s,
    hy_r,
    hs_s,
    hs_r,
    w_s,
    w_r,
    r1_s,
    r1_r,
    r2_s,
    r2_r,
    dx_s,
    dx_r,
    dz_s,
    dz_r,
    de_s,
    de_r,
    out_sem,
):
    r = lax.axis_index("req")
    h = lax.axis_index("head")
    z, x = r // NX, lax.rem(r, NX)
    y, c = h // 2, lax.rem(h, 2)

    def at_x(k):
        return lax.rem(x + k, NX)

    def at_z(k):
        return lax.rem(z + k, NZ)

    def dev_x(k):
        return (z * NX + at_x(k), h)

    def dev_z(k):
        return (at_z(k) * NX + x, h)

    def head_y(k):
        return lax.rem(y + k, NY) * 2 + c

    def dev_y(k):
        return (r, head_y(k))

    sibling = (r, y * 2 + 1 - c)

    def send(src, dst, s, d, device):
        return pltpu.make_async_remote_copy(
            src_ref=src, dst_ref=dst, send_sem=s, recv_sem=d, device_id=device, device_id_type=MESH
        )

    own = []
    for n in range(4):
        own.append(
            pltpu.make_async_copy(
                wq.at[:, pl.ds(n * COLS, COLS)], wg.at[n, pl.ds(z * 256, 256)], own_sem.at[n]
            )
        )
    own.append(
        pltpu.make_async_copy(wk, wg.at[4, pl.ds(z * 256, 256), pl.ds(0, HD)], own_sem.at[4])
    )
    own.append(
        pltpu.make_async_copy(wv, wg.at[4, pl.ds(z * 256, 256), pl.ds(HD, HD)], own_sem.at[5])
    )
    for copy in own:
        copy.start()

    barrier = pltpu.get_barrier_semaphore()
    for k in range(1, NX):
        pl.semaphore_signal(barrier, inc=1, device_id=dev_x(k), device_id_type=MESH)
    for k in range(1, NZ):
        pl.semaphore_signal(barrier, inc=1, device_id=dev_z(k), device_id_type=MESH)
    for k in (1, 3):
        pl.semaphore_signal(barrier, inc=1, device_id=dev_y(k), device_id_type=MESH)
    pl.semaphore_signal(barrier, inc=1, device_id=sibling, device_id_type=MESH)
    pl.semaphore_wait(barrier, 13)

    started = []

    def go(copy):
        copy.start()
        started.append(copy)
        return copy

    def h_at(row_x, head):
        return hg.at[
            pl.ds(pl.multiple_of(row_x * 256, 256), 256),
            pl.ds(pl.multiple_of(head * 256, 256), 256),
        ]

    hx = []
    for k in range(1, NX):
        cols = pl.ds(pl.multiple_of(at_x(k) * 256, 256), 256)
        hx.append(
            go(send(hid.at[:, cols], h_at(x, h), hx_s.at[k - 1], hx_r.at[k - 1], dev_x(k)))
        )
    own_h = pltpu.make_async_copy(
        hid.at[:, pl.ds(pl.multiple_of(x * 256, 256), 256)], h_at(x, h), own_sem.at[6]
    )
    own_h.start()

    def w_step(n, s):
        pair = []
        for way in range(2):
            if s > 1:
                w_copies[(n, s - 1, way)].wait_recv()
        for way in range(2):
            back = (NZ - (s - 1)) if way == 0 else (s - 1)
            block = at_z(back) * 256
            if s < 4:
                rows = pl.ds(pl.multiple_of(block, 256), 256)
            else:
                rows = pl.ds(pl.multiple_of(block + 128 * way, 128), 128)
            ref = wg.at[n, rows]
            i = (n * 4 + s - 1) * 2 + way
            pair.append(go(send(ref, ref, w_s.at[i], w_r.at[i], dev_z(1 if way == 0 else NZ - 1))))
        w_copies[(n, s, 0)], w_copies[(n, s, 1)] = pair

    w_copies = {}

    def w_slot(t):
        for n in range(CHUNKS):
            s = t - n
            if 1 <= s <= 4:
                if s == 1:
                    own[n].wait()
                    if n == 4:
                        own[5].wait()
                w_step(n, s)

    def w_finish(n):
        for way in range(2):
            w_copies[(n, 4, way)].wait_recv()

    w_slot(1)

    def pack(zt, carry):
        for k in range(NX):
            target = zt * NX + at_x(k)
            for rank in range(2):
                index = tab[target * 2 + rank]
                keys, values = dk[index], dv[index]
                if k == 0:
                    xr[x, rank, zt, 0] = keys
                    xr[x, rank, zt, 1] = values
                else:
                    xs[k - 1, rank, zt, 0] = keys
                    xs[k - 1, rank, zt, 1] = values
        return carry

    lax.fori_loop(0, NZ, pack, 0)

    def send_docs_x(rank):
        copies = []
        for k in range(1, NX):
            i = rank * 3 + k - 1
            copies.append(
                go(send(xs.at[k - 1, rank], xr.at[x, rank], dx_s.at[i], dx_r.at[i], dev_x(k)))
            )
        return copies

    w_slot(2)
    for copy in hx:
        copy.wait_recv()
    own_h.wait()

    def h_cols(head, rows=slice(0, 1024)):
        return hg.at[
            pl.ds(rows.start, rows.stop - rows.start), pl.ds(pl.multiple_of(head * 256, 256), 256)
        ]

    hy, hs = [], []
    for way, k in ((0, 1), (1, 3)):
        hy.append(go(send(h_cols(h), h_cols(h), hy_s.at[way], hy_r.at[way], dev_y(k))))
    hs.append(go(send(h_cols(h), h_cols(h), hs_s.at[0], hs_r.at[0], sibling)))
    docs_x = send_docs_x(0)
    w_slot(3)
    w_slot(4)
    for copy in hy:
        copy.wait_recv()
    top, bottom = slice(0, 512), slice(512, 1024)
    left, right = head_y(3), head_y(1)
    hy2 = [
        go(send(h_cols(left, top), h_cols(left, top), hy_s.at[2], hy_r.at[2], dev_y(1))),
        go(send(h_cols(right, bottom), h_cols(right, bottom), hy_s.at[3], hy_r.at[3], dev_y(3))),
    ]
    hs.append(go(send(h_cols(left), h_cols(left), hs_s.at[1], hs_r.at[1], sibling)))
    hs.append(go(send(h_cols(right), h_cols(right), hs_s.at[2], hs_r.at[2], sibling)))
    w_slot(5)
    for copy in hy2:
        copy.wait_recv()
    far = head_y(2)
    hs.append(go(send(h_cols(far), h_cols(far), hs_s.at[3], hs_r.at[3], sibling)))
    for copy in hs:
        copy.wait_recv()

    def product(n, k):
        block = lax.rem(x + k, NX)
        rows = pl.ds(pl.multiple_of(block * 256, 256), 256)
        part[n, block] = jnp.dot(hg[rows, :], wg[n], preferred_element_type=jnp.float32)

    r1_copies, r2_copies = {}, {}

    def multiply(n):
        w_finish(n)
        product(n, 2)
        far_x = at_x(2)
        r1_copies[n] = [
            go(
                send(
                    part.at[n, far_x, pl.ds(128 * way, 128)],
                    r1.at[n, way],
                    r1_s.at[n * 2 + way],
                    r1_r.at[n * 2 + way],
                    dev_x(1 if way == 0 else 3),
                )
            )
            for way in range(2)
        ]

        def rest(k, carry):
            product(n, k)
            return carry

        lax.fori_loop(3, 6, rest, 0)

    def second(n):
        for copy in r1_copies[n]:
            copy.wait_recv()
        part[n, at_x(1), pl.ds(0, 128)] = part[n, at_x(1), pl.ds(0, 128)] + r1[n, 0]
        part[n, at_x(3), pl.ds(128, 128)] = part[n, at_x(3), pl.ds(128, 128)] + r1[n, 1]
        r2_copies[n] = [
            go(
                send(
                    part.at[n, at_x(1 if way == 0 else 3)],
                    r2.at[n, way],
                    r2_s.at[n * 2 + way],
                    r2_r.at[n * 2 + way],
                    dev_x(1 if way == 0 else 3),
                )
            )
            for way in range(2)
        ]

    def third(n):
        for copy in r2_copies[n]:
            copy.wait_recv()
        total = (part[n, x] + r2[n, 0] + r2[n, 1]).astype(jnp.bfloat16)
        if n < 4:
            q_out[:, pl.ds(n * COLS, COLS)] = total
        else:
            nk_out[...] = total[:, :HD]
            nv_out[...] = total[:, HD:]

    multiply(0)
    w_slot(6)
    docs_x1 = send_docs_x(1)
    multiply(1)
    second(0)
    w_slot(7)
    multiply(2)
    second(1)
    third(0)
    w_slot(8)

    for copy in docs_x:
        copy.wait_recv()
    docs_z = []
    for k in (4, 3, 5, 2, 6, 1, 7):
        docs_z.append(
            go(
                send(
                    xr.at[:, 0, at_z(k)],
                    zr.at[z, pl.ds(0, 4)],
                    dz_s.at[k - 1],
                    dz_r.at[k - 1],
                    dev_z(k),
                )
            )
        )
    own_z = pltpu.make_async_copy(xr.at[:, 0, z], zr.at[z, pl.ds(0, 4)], own_sem.at[7])
    own_z.start()

    multiply(3)
    second(2)
    third(1)
    multiply(4)
    second(3)
    third(2)

    for copy in docs_x1:
        copy.wait_recv()

    def extra(zt, carry):
        chosen = exsel[zt]
        ex[zt] = xr[chosen, 1, zt]
        return carry

    lax.fori_loop(0, NZ, extra, 0)
    docs_e = []
    for k in (4, 3, 5, 2, 6, 1, 7):
        docs_e.append(
            go(send(ex.at[at_z(k)], zr.at[z, 4], de_s.at[k - 1], de_r.at[k - 1], dev_z(k)))
        )
    own_e = pltpu.make_async_copy(ex.at[z], zr.at[z, 4], own_sem.at[8])
    own_e.start()

    second(4)
    third(3)
    third(4)
    own_z.wait()
    own_e.wait()
    for copy in docs_z:
        copy.wait_recv()
    for copy in docs_e:
        copy.wait_recv()
    result = pltpu.make_async_copy(zr, docs_out, out_sem)
    result.start()
    for copy in started:
        copy.wait_send()
    result.wait()


def exchange(tab, exsel, hid, dk, dv, wq, wk, wv):
    vmem = pl.BlockSpec(memory_space=pltpu.VMEM)
    smem = pl.BlockSpec(memory_space=pltpu.SMEM)
    anym = pl.BlockSpec(memory_space=pl.ANY)
    dma = pltpu.SemaphoreType.DMA
    bf16, f32 = jnp.bfloat16, jnp.float32
    return pl.pallas_call(
        exchange_kernel,
        out_shape=(
            jax.ShapeDtypeStruct((256, 1024), bf16),
            jax.ShapeDtypeStruct((256, HD), bf16),
            jax.ShapeDtypeStruct((256, HD), bf16),
            jax.ShapeDtypeStruct((NZ, 5, 2, 128, HD), bf16),
        ),
        in_specs=[smem, smem, vmem, vmem, vmem, anym, anym, anym],
        out_specs=(vmem, vmem, vmem, anym),
        scratch_shapes=[
            pltpu.VMEM((1024, 2048), bf16),
            pltpu.VMEM((CHUNKS, 2048, COLS), bf16),
            pltpu.VMEM((CHUNKS, NX, 256, COLS), f32),
            pltpu.VMEM((CHUNKS, 2, 128, COLS), f32),
            pltpu.VMEM((CHUNKS, 2, 256, COLS), f32),
            pltpu.VMEM((3, 2, NZ, 2, 128, HD), bf16),
            pltpu.VMEM((NX, 2, NZ, 2, 128, HD), bf16),
            pltpu.VMEM((NZ, 2, 128, HD), bf16),
            pltpu.VMEM((NZ, 5, 2, 128, HD), bf16),
            dma((9,)),
            dma((3,)),
            dma((3,)),
            dma((4,)),
            dma((4,)),
            dma((4,)),
            dma((4,)),
            dma((40,)),
            dma((40,)),
            dma((10,)),
            dma((10,)),
            dma((10,)),
            dma((10,)),
            dma((6,)),
            dma((6,)),
            dma((7,)),
            dma((7,)),
            dma((7,)),
            dma((7,)),
            dma,
        ],
        compiler_params=pltpu.CompilerParams(
            collective_id=0, has_side_effects=True, vmem_limit_bytes=48 * 2**20
        ),
    )(tab, exsel, hid, dk, dv, wq, wk, wv)


def attention_kernel(
    where, rows, ids, kept, counts, q, nk, nv, docs, out, keys, values, bias
):
    request, pair = pl.program_id(0), pl.program_id(1)
    span = SLOTS * BLK

    @pl.when((request == 0) & (pair == 0))
    def _():
        hot = (ids[...] == lax.broadcasted_iota(jnp.int32, (2 * NDOC, 512), 1)).astype(jnp.bfloat16)
        blocks = jnp.dot(
            hot, kept[...].astype(jnp.float32).astype(jnp.bfloat16), preferred_element_type=jnp.float32
        )
        spread = (
            lax.broadcasted_iota(jnp.int32, (SLOTS, span), 1) // BLK
            == lax.broadcasted_iota(jnp.int32, (SLOTS, span), 0)
        ).astype(jnp.bfloat16)
        block = jnp.dot(
            blocks.astype(jnp.bfloat16), spread, preferred_element_type=jnp.float32
        ).astype(jnp.int32)
        count = jnp.dot(
            hot,
            jnp.broadcast_to(counts[...], (512, span)).astype(jnp.float32).astype(jnp.bfloat16),
            preferred_element_type=jnp.float32,
        ).astype(jnp.int32)
        token = lax.broadcasted_iota(jnp.int32, (2 * NDOC, span), 1)
        ref = lax.broadcasted_iota(jnp.int32, (2 * NDOC, span), 0)
        position = lax.rem(ref, NDOC) * (DOC_BLKS * BLK) + block * BLK + lax.rem(token, BLK)
        dead = (token // BLK >= count).astype(jnp.int32)
        first = ref < NDOC

        def compare(k, dead):
            row = jnp.where(first, rows[0, k], rows[1, k])
            return dead | (position == row).astype(jnp.int32)

        dead = lax.fori_loop(0, 128, compare, dead)
        shut = jnp.where(dead > 0, -jnp.inf, 0.0)
        for i in range(2):
            for j in range(NDOC):
                bias[i, :, pl.ds(j * span, span)] = shut[i * NDOC + j : i * NDOC + j + 1]
            bias[i, :, pl.ds(NDOC * span, 128)] = jnp.zeros((1, 128), jnp.float32)

    @pl.when(pair == 0)
    def _():
        for j in range(NDOC):
            slot = where[request * NDOC + j]
            keys[pl.ds(j * span, span)] = docs[slot, 0]
            values[pl.ds(j * span, span)] = docs[slot, 1]
        keys[pl.ds(NDOC * span, 128)] = nk[...]
        values[pl.ds(NDOC * span, 128)] = nv[...]

    scale = 1.0 / math.sqrt(HD)
    for g in range(2):
        cols = pl.ds(g * HD, HD)
        scores = lax.dot_general(
            q[:, cols], keys[...], (((1,), (1,)), ((), ())), preferred_element_type=jnp.float32
        )
        scores = scores * scale + bias[request]
        peak = jnp.max(scores, axis=-1, keepdims=True)
        weights = jnp.exp(scores - peak)
        probs = (weights / jnp.sum(weights, axis=-1, keepdims=True)).astype(jnp.bfloat16)
        out[:, cols] = jnp.dot(probs, values[...], preferred_element_type=jnp.float32).astype(
            jnp.bfloat16
        )


def attention(where, rows, ids, kept, counts, q, nk, nv, docs):
    smem = pl.BlockSpec(memory_space=pltpu.SMEM)
    vmem = pl.BlockSpec(memory_space=pltpu.VMEM)
    context = NDOC * SLOTS * BLK + 128
    return pl.pallas_call(
        attention_kernel,
        grid=(2, 4),
        out_shape=jax.ShapeDtypeStruct((256, 1024), jnp.bfloat16),
        in_specs=[
            smem,
            smem,
            vmem,
            vmem,
            vmem,
            pl.BlockSpec((128, 256), lambda i, p: (i, p)),
            pl.BlockSpec((128, HD), lambda i, p: (i, 0)),
            pl.BlockSpec((128, HD), lambda i, p: (i, 0)),
            vmem,
        ],
        out_specs=pl.BlockSpec((128, 256), lambda i, p: (i, p)),
        scratch_shapes=[
            pltpu.VMEM((context, HD), jnp.bfloat16),
            pltpu.VMEM((context, HD), jnp.bfloat16),
            pltpu.VMEM((2, 1, context), jnp.float32),
        ],
        compiler_params=pltpu.CompilerParams(vmem_limit_bytes=48 * 2**20),
    )(where, rows, ids, kept, counts, q, nk, nv, docs)


def shards(
    hidden,
    w_query,
    w_key,
    w_value,
    doc_keys,
    doc_values,
    slot_counts,
    kept_blocks,
    doc_ids,
    doc_place,
    recompute_rows,
):
    owners = lax.axis_size("req")
    mine = lax.axis_index("req")
    refs = 2 * NDOC
    my_z, my_x = mine // NX, lax.rem(mine, NX)
    flat = doc_ids.reshape(-1)
    placed = jnp.sum(
        jnp.where(flat[:, None] == jnp.arange(512, dtype=jnp.int32)[None, :], doc_place[None, :], 0),
        axis=1,
    ).reshape(owners, refs)
    owner_all, local_all = placed // 16, placed % 16
    order = jnp.arange(refs, dtype=jnp.int32)
    spare = refs * 16
    key = jnp.where(owner_all == mine, order[None, :] * 16 + local_all, spare)
    first = jnp.min(key, axis=1)
    second = jnp.min(jnp.where(key > first[:, None], key, spare), axis=1)
    tab = jnp.stack([first % 16, second % 16], axis=1).reshape(-1)
    held = jnp.sum(
        (owner_all[:, None, :] == jnp.arange(owners, dtype=jnp.int32)[None, :, None]).astype(jnp.int32),
        axis=2,
    )
    twice = (held > 1).reshape(owners, NZ, NX)
    crowded = jnp.any(jnp.sum(twice.astype(jnp.int32), axis=2) > 1)
    my_twice = lax.dynamic_index_in_dim(twice, my_z, 1, False)
    choice = jnp.max(jnp.where(my_twice, jnp.arange(NX, dtype=jnp.int32)[None, :], 0), axis=1)
    exsel = lax.dynamic_index_in_dim(choice.reshape(NZ, NX), my_x, 1, False)
    own_owner = lax.dynamic_index_in_dim(owner_all, mine, 0, False)
    later = jnp.any(
        (own_owner[:, None] == own_owner[None, :]) & (order[None, :] < order[:, None]), axis=1
    )
    where = (own_owner // NX) * 5 + jnp.where(later, 4, own_owner % NX)
    ids = lax.dynamic_slice_in_dim(doc_ids, mine * 2, 2, 0).reshape(refs, 1)

    def fast():
        q, nk, nv, docs = exchange(
            tab,
            exsel,
            hidden.reshape(256, -1),
            doc_keys.reshape(16, 128, HD),
            doc_values.reshape(16, 128, HD),
            w_query,
            w_key,
            w_value,
        )
        attended = attention(
            where,
            recompute_rows,
            ids,
            kept_blocks.reshape(512, SLOTS),
            slot_counts,
            q,
            nk,
            nv,
            docs.reshape(NZ * 5, 2, 128, HD),
        )
        return (
            attended.reshape(2, 128, 1024),
            nk.reshape(2, 128, HD),
            nv.reshape(2, 128, HD),
        )

    def slow():
        return general(
            hidden,
            w_query,
            w_key,
            w_value,
            doc_keys,
            doc_values,
            slot_counts,
            kept_blocks,
            doc_ids,
            doc_place,
            recompute_rows,
        )

    return lax.cond(crowded, slow, fast)


def solution(mesh):
    return jax.shard_map(
        shards,
        mesh=mesh,
        in_specs=(
            P("req", None, "head"),
            P("req", "head"),
            P("req", "head"),
            P("req", "head"),
            P("req", "head", None, None),
            P("req", "head", None, None),
            P(None, "head"),
            P(None, "head", None),
            P(),
            P(),
            P("req", None),
        ),
        out_specs=(P("req", None, "head"), P("req", None, "head"), P("req", None, "head")),
        check_vma=False,
    )
```

```python
import math

import jax
import jax.numpy as jnp
from jax import lax
from jax.experimental import pallas as pl
from jax.experimental.pallas import tpu as pltpu
from jax.sharding import PartitionSpec as P

QH = 64
KVH = 8
HD = 128
BLK = 16
DOC_BLKS = 16
SLOTS = 8
NDOC = 16


def attend(block_queries, context_keys, context_values, live, scale):
    scores = (
        jnp.einsum("rgd,kd->rgk", block_queries, context_keys, preferred_element_type=jnp.float32)
        * scale
    )
    scores = jnp.where(live[None, None, :], scores, -jnp.inf)
    peak = jnp.max(scores, axis=-1, keepdims=True)
    weights = jnp.exp(scores - peak)
    probs = (weights / jnp.sum(weights, axis=-1, keepdims=True)).astype(jnp.bfloat16)
    result = jnp.einsum("rgk,kd->rgd", probs, context_values, preferred_element_type=jnp.float32)
    return result.astype(jnp.bfloat16).reshape(block_queries.shape[0], -1)


def general(
    queries,
    keys_new,
    values_new,
    doc_keys,
    doc_values,
    slot_counts,
    kept_blocks,
    doc_ids,
    doc_place,
    recompute_rows,
):
    req_here, rows_req, heads_here = 2, queries.shape[0] // 2, 1
    group = QH // KVH
    span = SLOTS * BLK
    scale = 1.0 / math.sqrt(HD)
    owners = lax.axis_size("req")
    mine = lax.axis_index("req")
    docs_here = doc_keys.shape[0]
    refs = req_here * NDOC
    capacity = 2 * (refs // owners)
    placed = doc_place[doc_ids]
    owner_all = (placed // docs_here).reshape(owners, refs)
    local_all = (placed % docs_here).reshape(owners, refs)
    order = jnp.arange(refs, dtype=jnp.int32)
    earlier = (owner_all[:, :, None] == owner_all[:, None, :]) & (
        order[None, None, :] < order[None, :, None]
    )
    rank = jnp.sum(earlier.astype(jnp.int32), axis=2)
    slot_ids = jnp.arange(capacity, dtype=jnp.int32)
    match = (
        (owner_all == mine)[:, :, None] & (rank[:, :, None] == slot_ids[None, None, :])
    ).astype(jnp.int32)
    picked = jnp.sum(match * local_all[:, :, None], axis=1)
    used = jnp.sum(match, axis=1) > 0

    def pack(cache):
        selected = cache[picked]
        return jnp.where(used[:, :, None, None, None], selected, jnp.zeros_like(selected))

    got_keys = lax.all_to_all(pack(doc_keys), "req", split_axis=0, concat_axis=0, tiled=True)
    got_values = lax.all_to_all(pack(doc_values), "req", split_axis=0, concat_axis=0, tiled=True)
    own_owner = lax.dynamic_index_in_dim(owner_all, mine, 0, False)
    own_rank = lax.dynamic_index_in_dim(rank, mine, 0, False)
    where_row = own_owner * capacity + own_rank
    tail = got_keys.shape[2:]
    fetched_keys = got_keys.reshape((owners * capacity,) + tail)[where_row].reshape(
        (req_here, NDOC) + tail
    )
    fetched_values = got_values.reshape((owners * capacity,) + tail)[where_row].reshape(
        (req_here, NDOC) + tail
    )
    queries = queries.reshape(req_here, rows_req, heads_here, group, HD)
    keys_new = keys_new.reshape(req_here, rows_req, heads_here, HD)
    values_new = values_new.reshape(req_here, rows_req, heads_here, HD)
    my_ids = lax.dynamic_slice_in_dim(doc_ids, mine * req_here, req_here, 0)
    offsets = jnp.arange(NDOC, dtype=jnp.int32)[:, None, None] * (DOC_BLKS * BLK)
    inner = jnp.arange(BLK, dtype=jnp.int32)[None, None, :]
    slot_index = jnp.arange(SLOTS, dtype=jnp.int32)[None, :, None]
    block_rows = 128
    request_outputs = []
    for request in range(req_here):
        ids = my_ids[request]
        positions = recompute_rows[request]
        blocks = kept_blocks[ids, 0]
        count_here = slot_counts[ids, 0]
        key_pos = (offsets + blocks[:, :, None] * BLK + inner).reshape(-1)
        valid = (slot_index < count_here[:, None, None]) & (inner >= 0)
        replaced = jnp.any(key_pos[:, None] == positions[None, :], axis=1)
        live = jnp.concatenate(
            [valid.reshape(-1) & jnp.logical_not(replaced), jnp.ones((rows_req,), bool)]
        )
        context_keys = jnp.concatenate(
            [fetched_keys[request, :, 0].reshape(NDOC * span, HD), keys_new[request, :, 0]], axis=0
        )
        context_values = jnp.concatenate(
            [fetched_values[request, :, 0].reshape(NDOC * span, HD), values_new[request, :, 0]],
            axis=0,
        )
        query_blocks = queries[request, :, 0].reshape(rows_req // block_rows, block_rows, group, HD)
        result = lax.map(
            lambda block_queries: attend(block_queries, context_keys, context_values, live, scale),
            query_blocks,
        )
        head_outputs = result.reshape(rows_req, group * HD)
        request_outputs.append(head_outputs)
    return jnp.stack(request_outputs, axis=0)


MESH = pl.DeviceIdType.MESH
NX, NZ, NY = 4, 8, 4
COLS = 256
CHUNKS = 5


def exchange_kernel(
    rows,
    place,
    ids,
    kept,
    counts,
    hid,
    dk_in,
    dv_in,
    wq,
    wk,
    wv,
    out,
    q_out,
    nk_out,
    nv_out,
    flag,
    placed,
    table,
    tab,
    dk,
    dv,
    keys,
    values,
    bias,
    points,
    peaks,
    hg,
    wg,
    part,
    r1,
    r2,
    xs,
    xr,
    xr1,
    ex,
    zr,
    own_sem,
    hx_s,
    hx_r,
    hy_s,
    hy_r,
    hs_s,
    hs_r,
    w_s,
    w_r,
    r1_s,
    r1_r,
    r2_s,
    r2_r,
    dx_s,
    dx_r,
    dz_s,
    dz_r,
    de_s,
    de_r,
):
    r = lax.axis_index("req")
    h = lax.axis_index("head")
    z, x = r // NX, lax.rem(r, NX)
    y, c = h // 2, lax.rem(h, 2)

    def at_x(k):
        return lax.rem(x + k, NX)

    def at_z(k):
        return lax.rem(z + k, NZ)

    def dev_x(k):
        return (z * NX + at_x(k), h)

    def dev_z(k):
        return (at_z(k) * NX + x, h)

    def head_y(k):
        return lax.rem(y + k, NY) * 2 + c

    def dev_y(k):
        return (r, head_y(k))

    sibling = (r, y * 2 + 1 - c)

    def send(src, dst, s, d, device):
        return pltpu.make_async_remote_copy(
            src_ref=src, dst_ref=dst, send_sem=s, recv_sem=d, device_id=device, device_id_type=MESH
        )

    docs_in = [
        pltpu.make_async_copy(dk_in, dk, own_sem.at[9]),
        pltpu.make_async_copy(dv_in, dv, own_sem.at[10]),
    ]
    own = []
    for n in range(4):
        own.append(
            pltpu.make_async_copy(
                wq.at[:, pl.ds(n * COLS, COLS)], wg.at[n, pl.ds(z * 256, 256)], own_sem.at[n]
            )
        )
    own.append(
        pltpu.make_async_copy(wk, wg.at[4, pl.ds(z * 256, 256), pl.ds(0, HD)], own_sem.at[4])
    )
    own.append(
        pltpu.make_async_copy(wv, wg.at[4, pl.ds(z * 256, 256), pl.ds(HD, HD)], own_sem.at[5])
    )
    for copy in own + docs_in:
        copy.start()

    barrier = pltpu.get_barrier_semaphore()
    for k in range(1, NX):
        pl.semaphore_signal(barrier, inc=1, device_id=dev_x(k), device_id_type=MESH)
    for k in range(1, NZ):
        pl.semaphore_signal(barrier, inc=1, device_id=dev_z(k), device_id_type=MESH)
    for k in (1, 3):
        pl.semaphore_signal(barrier, inc=1, device_id=dev_y(k), device_id_type=MESH)
    pl.semaphore_signal(barrier, inc=1, device_id=sibling, device_id_type=MESH)
    pl.semaphore_wait(barrier, 13)

    started = []

    def go(copy):
        copy.start()
        started.append(copy)
        return copy

    def mask():
        span = SLOTS * BLK
        refs = 2 * NDOC
        hot = (
            lax.broadcasted_iota(jnp.int32, (512, refs), 0)
            == jnp.broadcast_to(ids[pl.ds(r, 1), :], (512, refs))
        ).astype(jnp.float32)
        hot = hot.astype(jnp.bfloat16)

        def whole(a):
            return a.astype(jnp.float32).astype(jnp.bfloat16)

        blocks = jnp.dot(whole(kept[...]), hot, preferred_element_type=jnp.float32)
        spread = whole(
            (
                lax.broadcasted_iota(jnp.int32, (SLOTS, span), 1) // BLK
                == lax.broadcasted_iota(jnp.int32, (SLOTS, span), 0)
            ).astype(jnp.int32)
        )
        across = (((0,), (0,)), ((), ()))
        block = lax.dot_general(
            blocks.astype(jnp.bfloat16), spread, across, preferred_element_type=jnp.float32
        ).astype(jnp.int32)
        held = jnp.dot(
            whole(jnp.broadcast_to(counts[...], (8, 512))), hot, preferred_element_type=jnp.float32
        )
        eighth = jnp.full((8, span), 0.125, jnp.bfloat16)
        count = lax.dot_general(
            held.astype(jnp.bfloat16), eighth, across, preferred_element_type=jnp.float32
        ).astype(jnp.int32)
        token = lax.broadcasted_iota(jnp.int32, (refs, span), 1)
        ref = lax.broadcasted_iota(jnp.int32, (refs, span), 0)
        position = lax.rem(ref, NDOC) * (DOC_BLKS * BLK) + block * BLK + lax.rem(token, BLK)
        dead = (token // BLK >= count).astype(jnp.int32)
        first = ref < NDOC

        def compare(k, dead):
            row = jnp.where(first, rows[0, k], rows[1, k])
            return dead | (position == row).astype(jnp.int32)

        dead = lax.fori_loop(0, 128, compare, dead)
        shut = jnp.where(dead > 0, -jnp.inf, 0.0)
        for i in range(2):
            for j in range(NDOC):
                bias[i, :, pl.ds(j * span, span)] = shut[i * NDOC + j : i * NDOC + j + 1]
            bias[i, :, pl.ds(NDOC * span, 128)] = jnp.zeros((1, 128), jnp.float32)

    def h_at(row_x, head):
        return hg.at[
            pl.ds(pl.multiple_of(row_x * 256, 256), 256),
            pl.ds(pl.multiple_of(head * 256, 256), 256),
        ]

    hx = []
    for k in range(1, NX):
        cols = pl.ds(pl.multiple_of(at_x(k) * 256, 256), 256)
        hx.append(
            go(send(hid.at[:, cols], h_at(x, h), hx_s.at[k - 1], hx_r.at[k - 1], dev_x(k)))
        )
    own_h = pltpu.make_async_copy(
        hid.at[:, pl.ds(pl.multiple_of(x * 256, 256), 256)], h_at(x, h), own_sem.at[6]
    )
    own_h.start()

    def w_step(n, s):
        pair = []
        for way in range(2):
            if s > 1:
                w_copies[(n, s - 1, way)].wait_recv()
        for way in range(2):
            back = (NZ - (s - 1)) if way == 0 else (s - 1)
            block = at_z(back) * 256
            if s < 4:
                rows = pl.ds(pl.multiple_of(block, 256), 256)
            else:
                rows = pl.ds(pl.multiple_of(block + 128 * way, 128), 128)
            ref = wg.at[n, rows]
            i = (n * 4 + s - 1) * 2 + way
            pair.append(go(send(ref, ref, w_s.at[i], w_r.at[i], dev_z(1 if way == 0 else NZ - 1))))
        w_copies[(n, s, 0)], w_copies[(n, s, 1)] = pair

    w_copies = {}

    lead = (0, 0, 1, 2, 3)

    def w_slot(t):
        for n in range(CHUNKS):
            s = t - lead[n]
            if 1 <= s <= 4:
                if s == 1:
                    own[n].wait()
                    if n == 4:
                        own[5].wait()
                w_step(n, s)

    def w_finish(n):
        for way in range(2):
            w_copies[(n, 4, way)].wait_recv()

    w_slot(1)

    def look_up(d, found):
        return jnp.where(ids[...] == d, place[d], found)

    found = lax.fori_loop(0, 512, look_up, jnp.zeros((32, 32), jnp.int32), unroll=8)
    placed[...] = found
    owner, local = found // 16, lax.rem(found, 16)
    order = lax.broadcasted_iota(jnp.int32, (32, 32), 1)
    line = lax.broadcasted_iota(jnp.int32, (32, 32), 0)
    spare = 32 * 16
    key = jnp.where(owner == r, order * 16 + local, spare)
    first = jnp.min(key, axis=1, keepdims=True)
    second_key = jnp.min(jnp.where(key > first, key, spare), axis=1, keepdims=True)
    choice = jnp.zeros((32, 1), jnp.int32)
    worst = jnp.zeros((32, 1), jnp.int32)
    for zo in range(NZ):
        doubled = jnp.zeros((32, 1), jnp.int32)
        pick = jnp.zeros((32, 1), jnp.int32)
        for xo in range(NX):
            held = jnp.sum((owner == zo * NX + xo).astype(jnp.int32), axis=1, keepdims=True)
            twice = (held > 1).astype(jnp.int32)
            doubled = doubled + twice
            pick = jnp.maximum(pick, twice * xo)
        worst = jnp.maximum(worst, doubled)
        choice = jnp.where(z == zo, pick, choice)
    worst = jnp.broadcast_to(jnp.max(worst, axis=0, keepdims=True), (32, 1))
    mine_row = placed[pl.ds(r, 1), :] // 16
    mine_wide = jnp.broadcast_to(mine_row, (32, 32))
    mine_col = jnp.sum(jnp.where(order == line, mine_wide, 0), axis=1, keepdims=True)
    later = jnp.max(
        ((mine_wide == mine_col) & (order < line)).astype(jnp.int32), axis=1, keepdims=True
    )
    slot = (mine_col // NX) * 5 + jnp.where(later > 0, 4, lax.rem(mine_col, NX))
    lane = lax.broadcasted_iota(jnp.int32, (32, 128), 1)
    table[...] = jnp.where(
        lane == 0,
        lax.rem(first, 16),
        jnp.where(lane == 1, lax.rem(second_key, 16), jnp.where(lane == 2, choice, jnp.where(lane == 3, slot, worst))),
    )
    to_scalars = pltpu.make_async_copy(table, tab, own_sem.at[11])
    to_scalars.start()
    to_scalars.wait()
    flag[0, 0] = tab[0, 4]
    for copy in docs_in:
        copy.wait()

    def pack(rank):
        def one(zt, carry):
            for k in range(NX):
                index = tab[zt * NX + at_x(k), rank]
                if k == 0:
                    here = xr1 if rank else xr
                    here[x, zt, 0] = dk[index]
                    here[x, zt, 1] = dv[index]
                else:
                    xs[k - 1, rank, zt, 0] = dk[index]
                    xs[k - 1, rank, zt, 1] = dv[index]
            return carry

        lax.fori_loop(0, NZ, one, 0)

    def send_docs_x(rank):
        there = (xr1 if rank else xr).at[x]
        copies = []
        for k in range(1, NX):
            i = rank * 3 + k - 1
            copies.append(
                go(send(xs.at[k - 1, rank], there, dx_s.at[i], dx_r.at[i], dev_x(k)))
            )
        return copies

    pack(0)
    docs_x = send_docs_x(0)
    w_slot(2)
    pack(1)
    for copy in hx:
        copy.wait_recv()
    own_h.wait()

    def h_cols(head, rows=slice(0, 1024)):
        return hg.at[
            pl.ds(rows.start, rows.stop - rows.start), pl.ds(pl.multiple_of(head * 256, 256), 256)
        ]

    hy, hs = [], []
    for way, k in ((0, 1), (1, 3)):
        hy.append(go(send(h_cols(h), h_cols(h), hy_s.at[way], hy_r.at[way], dev_y(k))))
    hs.append(go(send(h_cols(h), h_cols(h), hs_s.at[0], hs_r.at[0], sibling)))
    w_slot(3)
    mask()
    w_slot(4)
    docs_x1 = send_docs_x(1)
    for copy in hy:
        copy.wait_recv()
    top, bottom = slice(0, 512), slice(512, 1024)
    left, right = head_y(3), head_y(1)
    hy2 = [
        go(send(h_cols(left, top), h_cols(left, top), hy_s.at[2], hy_r.at[2], dev_y(1))),
        go(send(h_cols(right, bottom), h_cols(right, bottom), hy_s.at[3], hy_r.at[3], dev_y(3))),
    ]
    hs.append(go(send(h_cols(left), h_cols(left), hs_s.at[1], hs_r.at[1], sibling)))
    hs.append(go(send(h_cols(right), h_cols(right), hs_s.at[2], hs_r.at[2], sibling)))
    w_slot(5)
    for copy in hy2:
        copy.wait_recv()
    far = head_y(2)
    hs.append(go(send(h_cols(far), h_cols(far), hs_s.at[3], hs_r.at[3], sibling)))
    for copy in hs:
        copy.wait_recv()

    def product(n, k):
        block = lax.rem(x + k, NX)
        rows = pl.ds(pl.multiple_of(block * 256, 256), 256)
        part[n, block] = jnp.dot(hg[rows, :], wg[n], preferred_element_type=jnp.float32)

    r1_copies, r2_copies = {}, {}

    def multiply(n):
        w_finish(n)
        product(n, 2)
        far_x = at_x(2)
        r1_copies[n] = [
            go(
                send(
                    part.at[n, far_x, pl.ds(128 * way, 128)],
                    r1.at[n, way],
                    r1_s.at[n * 2 + way],
                    r1_r.at[n * 2 + way],
                    dev_x(1 if way == 0 else 3),
                )
            )
            for way in range(2)
        ]

        def rest(k, carry):
            product(n, k)
            return carry

        lax.fori_loop(3, 6, rest, 0)

    def second(n):
        for copy in r1_copies[n]:
            copy.wait_recv()
        part[n, at_x(1), pl.ds(0, 128)] = part[n, at_x(1), pl.ds(0, 128)] + r1[n, 0]
        part[n, at_x(3), pl.ds(128, 128)] = part[n, at_x(3), pl.ds(128, 128)] + r1[n, 1]
        r2_copies[n] = [
            go(
                send(
                    part.at[n, at_x(1 if way == 0 else 3)],
                    r2.at[n, way],
                    r2_s.at[n * 2 + way],
                    r2_r.at[n * 2 + way],
                    dev_x(1 if way == 0 else 3),
                )
            )
            for way in range(2)
        ]

    def third(n):
        for copy in r2_copies[n]:
            copy.wait_recv()
        total = (part[n, x] + r2[n, 0] + r2[n, 1]).astype(jnp.bfloat16)
        if n < 4:
            for i in range(2):
                for g in range(2):
                    q_out[pl.ds(i * 1024 + (2 * n + g) * 128, 128)] = total[
                        i * 128 : (i + 1) * 128, g * HD : (g + 1) * HD
                    ]
        else:
            nk_out[...] = total[:, :HD]
            nv_out[...] = total[:, HD:]

    w_slot(6)
    multiply(0)
    w_slot(7)
    for copy in docs_x:
        copy.wait_recv()
    docs_z = []
    for k in (4, 3, 5, 2, 6, 1, 7):
        docs_z.append(
            go(
                send(
                    xr.at[:, at_z(k)],
                    zr.at[z, pl.ds(0, 4)],
                    dz_s.at[k - 1],
                    dz_r.at[k - 1],
                    dev_z(k),
                )
            )
        )
    own_z = pltpu.make_async_copy(xr.at[:, z], zr.at[z, pl.ds(0, 4)], own_sem.at[7])
    own_z.start()

    multiply(1)
    multiply(2)
    second(0)
    multiply(3)
    second(1)
    multiply(4)
    for copy in docs_x1:
        copy.wait_recv()

    def extra(zt, carry):
        chosen = tab[zt * NX + x, 2]
        ex[zt] = xr1[chosen, zt]
        return carry

    lax.fori_loop(0, NZ, extra, 0)
    docs_e = []
    for k in (4, 3, 5, 2, 6, 1, 7):
        docs_e.append(
            go(send(ex.at[at_z(k)], zr.at[z, 4], de_s.at[k - 1], de_r.at[k - 1], dev_z(k)))
        )
    own_e = pltpu.make_async_copy(ex.at[z], zr.at[z, 4], own_sem.at[8])
    own_e.start()


    second(2)
    third(0)
    second(3)
    third(1)
    second(4)
    third(2)
    third(3)
    third(4)
    own_z.wait()
    own_e.wait()
    for copy in docs_z:
        copy.wait_recv()
    for copy in docs_e:
        copy.wait_recv()
    span = SLOTS * BLK
    for i in range(2):

        def fetch(j, carry):
            slot = tab[i * NDOC + j, 3]
            at = pl.ds(pl.multiple_of(j * span, span), span)
            keys[i, at] = zr[slot // 5, lax.rem(slot, 5), 0]
            values[i, at] = zr[slot // 5, lax.rem(slot, 5), 1]
            return carry

        lax.fori_loop(0, NDOC, fetch, 0)
        keys[i, pl.ds(NDOC * span, 128)] = nk_out[pl.ds(i * 128, 128)]
        values[i, pl.ds(NDOC * span, 128)] = nv_out[pl.ds(i * 128, 128)]

    factor = math.log2(math.e) / math.sqrt(HD)

    def score(step, side):
        i = step // 4
        at = pl.ds(pl.multiple_of(step * 256, 256), 256)
        scores = lax.dot_general(
            q_out[at], keys[i], (((1,), (1,)), ((), ())), preferred_element_type=jnp.float32
        )
        scores = scores * factor + bias[i]
        points[side] = scores
        peaks[side] = jnp.broadcast_to(jnp.max(scores, axis=-1, keepdims=True), (256, 128))

    def weigh(step, side):
        i, p = step // 4, lax.rem(step, 4)
        weights = jnp.exp2(points[side] - peaks[side][:, :1])
        share = 1.0 / jnp.sum(weights, axis=-1, keepdims=True)
        probs = (weights * share).astype(jnp.bfloat16)
        result = jnp.dot(probs, values[i], preferred_element_type=jnp.float32).astype(jnp.bfloat16)
        at = pl.ds(pl.multiple_of(i * 128, 128), 128)
        for g in range(2):
            cols = pl.ds(pl.multiple_of(p * 256 + g * HD, HD), HD)
            out[at, cols] = result[g * 128 : (g + 1) * 128]

    score(0, 0)

    def attend_two(k, carry):
        score(2 * k + 1, 1)
        weigh(2 * k, 0)
        score(lax.rem(2 * k + 2, 8), 0)
        weigh(2 * k + 1, 1)
        return carry

    lax.fori_loop(0, 4, attend_two, 0)
    for copy in started:
        copy.wait_send()


def fused(rows, place, ids, kept, counts, hid, dk, dv, wq, wk, wv):
    vmem = pl.BlockSpec(memory_space=pltpu.VMEM)
    smem = pl.BlockSpec(memory_space=pltpu.SMEM)
    anym = pl.BlockSpec(memory_space=pl.ANY)
    dma = pltpu.SemaphoreType.DMA
    bf16, f32 = jnp.bfloat16, jnp.float32
    context = NDOC * SLOTS * BLK + 128
    return pl.pallas_call(
        exchange_kernel,
        out_shape=(
            jax.ShapeDtypeStruct((256, 1024), bf16),
            jax.ShapeDtypeStruct((2048, HD), bf16),
            jax.ShapeDtypeStruct((256, HD), bf16),
            jax.ShapeDtypeStruct((256, HD), bf16),
            jax.ShapeDtypeStruct((1, 1), jnp.int32),
        ),
        in_specs=[smem, smem, vmem, vmem, vmem, anym, anym, anym, anym, anym, anym],
        out_specs=(vmem, vmem, vmem, vmem, smem),
        scratch_shapes=[
            pltpu.VMEM((32, 32), jnp.int32),
            pltpu.VMEM((32, 128), jnp.int32),
            pltpu.SMEM((32, 128), jnp.int32),
            pltpu.VMEM((16, 128, HD), bf16),
            pltpu.VMEM((16, 128, HD), bf16),
            pltpu.VMEM((2, context, HD), bf16),
            pltpu.VMEM((2, context, HD), bf16),
            pltpu.VMEM((2, 1, context), f32),
            pltpu.VMEM((2, 256, context), f32),
            pltpu.VMEM((2, 256, 128), f32),
            pltpu.VMEM((1024, 2048), bf16),
            pltpu.VMEM((CHUNKS, 2048, COLS), bf16),
            pltpu.VMEM((CHUNKS, NX, 256, COLS), f32),
            pltpu.VMEM((CHUNKS, 2, 128, COLS), f32),
            pltpu.VMEM((CHUNKS, 2, 256, COLS), f32),
            pltpu.VMEM((3, 2, NZ, 2, 128, HD), bf16),
            pltpu.VMEM((NX, NZ, 2, 128, HD), bf16),
            pltpu.VMEM((NX, NZ, 2, 128, HD), bf16),
            pltpu.VMEM((NZ, 2, 128, HD), bf16),
            pltpu.VMEM((NZ, 5, 2, 128, HD), bf16),
            dma((12,)),
            dma((3,)),
            dma((3,)),
            dma((4,)),
            dma((4,)),
            dma((4,)),
            dma((4,)),
            dma((40,)),
            dma((40,)),
            dma((10,)),
            dma((10,)),
            dma((10,)),
            dma((10,)),
            dma((6,)),
            dma((6,)),
            dma((7,)),
            dma((7,)),
            dma((7,)),
            dma((7,)),
        ],
        compiler_params=pltpu.CompilerParams(
            collective_id=0, has_side_effects=True, vmem_limit_bytes=60 * 2**20
        ),
    )(rows, place, ids, kept, counts, hid, dk, dv, wq, wk, wv)


def shards(
    hidden,
    w_query,
    w_key,
    w_value,
    doc_keys,
    doc_values,
    slot_counts,
    kept_blocks,
    doc_ids,
    doc_place,
    recompute_rows,
):
    owners = lax.axis_size("req")
    refs = 2 * NDOC
    ids = doc_ids.reshape(owners, refs)
    attended, queries, keys_new, values_new, flag = fused(
        recompute_rows,
        doc_place,
        ids,
        kept_blocks.reshape(512, SLOTS).T,
        slot_counts.T,
        hidden.reshape(256, -1),
        doc_keys.reshape(16, 128, HD),
        doc_values.reshape(16, 128, HD),
        w_query,
        w_key,
        w_value,
    )

    def again():
        return general(
            queries.reshape(2, 8, 128, HD).transpose(0, 2, 1, 3).reshape(256, 1024),
            keys_new,
            values_new,
            doc_keys,
            doc_values,
            slot_counts,
            kept_blocks,
            doc_ids,
            doc_place,
            recompute_rows,
        ).reshape(256, 1024)

    attended = lax.cond(flag[0, 0] > 1, again, lambda: attended)
    return (
        attended.reshape(2, 128, 1024),
        keys_new.reshape(2, 128, HD),
        values_new.reshape(2, 128, HD),
    )


def solution(mesh):
    return jax.shard_map(
        shards,
        mesh=mesh,
        in_specs=(
            P("req", None, "head"),
            P("req", "head"),
            P("req", "head"),
            P("req", "head"),
            P("req", "head", None, None),
            P("req", "head", None, None),
            P(None, "head"),
            P(None, "head", None),
            P(),
            P(),
            P("req", None),
        ),
        out_specs=(P("req", None, "head"), P("req", None, "head"), P("req", None, "head")),
        check_vma=False,
    )
```

```python
import math

import jax
import jax.numpy as jnp
from jax import lax
from jax.experimental import pallas as pl
from jax.experimental.pallas import tpu as pltpu
from jax.sharding import PartitionSpec as P

QH = 64
KVH = 8
HD = 128
BLK = 16
DOC_BLKS = 16
SLOTS = 8
NDOC = 16


def attend(block_queries, context_keys, context_values, live, scale):
    scores = (
        jnp.einsum("rgd,kd->rgk", block_queries, context_keys, preferred_element_type=jnp.float32)
        * scale
    )
    scores = jnp.where(live[None, None, :], scores, -jnp.inf)
    peak = jnp.max(scores, axis=-1, keepdims=True)
    weights = jnp.exp(scores - peak)
    probs = (weights / jnp.sum(weights, axis=-1, keepdims=True)).astype(jnp.bfloat16)
    result = jnp.einsum("rgk,kd->rgd", probs, context_values, preferred_element_type=jnp.float32)
    return result.astype(jnp.bfloat16).reshape(block_queries.shape[0], -1)


def general(
    queries,
    keys_new,
    values_new,
    doc_keys,
    doc_values,
    slot_counts,
    kept_blocks,
    doc_ids,
    doc_place,
    recompute_rows,
):
    req_here, rows_req, heads_here = 2, queries.shape[0] // 2, 1
    group = QH // KVH
    span = SLOTS * BLK
    scale = 1.0 / math.sqrt(HD)
    owners = lax.axis_size("req")
    mine = lax.axis_index("req")
    docs_here = doc_keys.shape[0]
    refs = req_here * NDOC
    capacity = 2 * (refs // owners)
    placed = doc_place[doc_ids]
    owner_all = (placed // docs_here).reshape(owners, refs)
    local_all = (placed % docs_here).reshape(owners, refs)
    order = jnp.arange(refs, dtype=jnp.int32)
    earlier = (owner_all[:, :, None] == owner_all[:, None, :]) & (
        order[None, None, :] < order[None, :, None]
    )
    rank = jnp.sum(earlier.astype(jnp.int32), axis=2)
    slot_ids = jnp.arange(capacity, dtype=jnp.int32)
    match = (
        (owner_all == mine)[:, :, None] & (rank[:, :, None] == slot_ids[None, None, :])
    ).astype(jnp.int32)
    picked = jnp.sum(match * local_all[:, :, None], axis=1)
    used = jnp.sum(match, axis=1) > 0

    def pack(cache):
        selected = cache[picked]
        return jnp.where(used[:, :, None, None, None], selected, jnp.zeros_like(selected))

    got_keys = lax.all_to_all(pack(doc_keys), "req", split_axis=0, concat_axis=0, tiled=True)
    got_values = lax.all_to_all(pack(doc_values), "req", split_axis=0, concat_axis=0, tiled=True)
    own_owner = lax.dynamic_index_in_dim(owner_all, mine, 0, False)
    own_rank = lax.dynamic_index_in_dim(rank, mine, 0, False)
    where_row = own_owner * capacity + own_rank
    tail = got_keys.shape[2:]
    fetched_keys = got_keys.reshape((owners * capacity,) + tail)[where_row].reshape(
        (req_here, NDOC) + tail
    )
    fetched_values = got_values.reshape((owners * capacity,) + tail)[where_row].reshape(
        (req_here, NDOC) + tail
    )
    queries = queries.reshape(req_here, rows_req, heads_here, group, HD)
    keys_new = keys_new.reshape(req_here, rows_req, heads_here, HD)
    values_new = values_new.reshape(req_here, rows_req, heads_here, HD)
    my_ids = lax.dynamic_slice_in_dim(doc_ids, mine * req_here, req_here, 0)
    offsets = jnp.arange(NDOC, dtype=jnp.int32)[:, None, None] * (DOC_BLKS * BLK)
    inner = jnp.arange(BLK, dtype=jnp.int32)[None, None, :]
    slot_index = jnp.arange(SLOTS, dtype=jnp.int32)[None, :, None]
    block_rows = 128
    request_outputs = []
    for request in range(req_here):
        ids = my_ids[request]
        positions = recompute_rows[request]
        blocks = kept_blocks[ids, 0]
        count_here = slot_counts[ids, 0]
        key_pos = (offsets + blocks[:, :, None] * BLK + inner).reshape(-1)
        valid = (slot_index < count_here[:, None, None]) & (inner >= 0)
        replaced = jnp.any(key_pos[:, None] == positions[None, :], axis=1)
        live = jnp.concatenate(
            [valid.reshape(-1) & jnp.logical_not(replaced), jnp.ones((rows_req,), bool)]
        )
        context_keys = jnp.concatenate(
            [fetched_keys[request, :, 0].reshape(NDOC * span, HD), keys_new[request, :, 0]], axis=0
        )
        context_values = jnp.concatenate(
            [fetched_values[request, :, 0].reshape(NDOC * span, HD), values_new[request, :, 0]],
            axis=0,
        )
        query_blocks = queries[request, :, 0].reshape(rows_req // block_rows, block_rows, group, HD)
        result = lax.map(
            lambda block_queries: attend(block_queries, context_keys, context_values, live, scale),
            query_blocks,
        )
        head_outputs = result.reshape(rows_req, group * HD)
        request_outputs.append(head_outputs)
    return jnp.stack(request_outputs, axis=0)


MESH = pl.DeviceIdType.MESH
NX, NZ, NY = 4, 8, 4
COLS = 256
CHUNKS = 5


def exchange_kernel(
    rows,
    place,
    ids,
    kept,
    counts,
    hid,
    dk_in,
    dv_in,
    wq,
    wk,
    wv,
    out,
    q_out,
    nk_out,
    nv_out,
    flag,
    placed,
    table,
    tab,
    dk,
    dv,
    keys,
    values,
    bias,
    points,
    shares,
    hg,
    wg,
    part,
    r1,
    r2,
    xs,
    xr,
    xr1,
    ex,
    inbox,
    zk,
    zv,
    own_sem,
    hx_s,
    hx_r,
    hy_s,
    hy_r,
    hs_s,
    hs_r,
    w_s,
    w_r,
    r1_s,
    r1_r,
    r2_s,
    r2_r,
    dx_s,
    dx_r,
    dz_s,
    dz_r,
    de_s,
    de_r,
):
    r = lax.axis_index("req")
    h = lax.axis_index("head")
    z, x = r // NX, lax.rem(r, NX)
    y, c = h // 2, lax.rem(h, 2)

    def at_x(k):
        return lax.rem(x + k, NX)

    def at_z(k):
        return lax.rem(z + k, NZ)

    def dev_x(k):
        return (z * NX + at_x(k), h)

    def dev_z(k):
        return (at_z(k) * NX + x, h)

    def head_y(k):
        return lax.rem(y + k, NY) * 2 + c

    def dev_y(k):
        return (r, head_y(k))

    sibling = (r, y * 2 + 1 - c)

    def send(src, dst, s, d, device):
        return pltpu.make_async_remote_copy(
            src_ref=src, dst_ref=dst, send_sem=s, recv_sem=d, device_id=device, device_id_type=MESH
        )

    docs_in = [
        pltpu.make_async_copy(dk_in, dk, own_sem.at[9]),
        pltpu.make_async_copy(dv_in, dv, own_sem.at[10]),
    ]
    own = []
    own.append(
        pltpu.make_async_copy(wk, wg.at[0, pl.ds(z * 256, 256), pl.ds(0, HD)], own_sem.at[0])
    )
    own.append(
        pltpu.make_async_copy(wv, wg.at[0, pl.ds(z * 256, 256), pl.ds(HD, HD)], own_sem.at[5])
    )
    for n in range(4):
        own.append(
            pltpu.make_async_copy(
                wq.at[:, pl.ds(n * COLS, COLS)],
                wg.at[n + 1, pl.ds(z * 256, 256)],
                own_sem.at[n + 1],
            )
        )
    for copy in own + docs_in:
        copy.start()

    barrier = pltpu.get_barrier_semaphore()
    for k in range(1, NX):
        pl.semaphore_signal(barrier, inc=1, device_id=dev_x(k), device_id_type=MESH)
    for k in range(1, NZ):
        pl.semaphore_signal(barrier, inc=1, device_id=dev_z(k), device_id_type=MESH)
    for k in (1, 3):
        pl.semaphore_signal(barrier, inc=1, device_id=dev_y(k), device_id_type=MESH)
    pl.semaphore_signal(barrier, inc=1, device_id=sibling, device_id_type=MESH)
    pl.semaphore_wait(barrier, 13)

    started = []

    def go(copy):
        copy.start()
        started.append(copy)
        return copy

    def mask():
        span = SLOTS * BLK
        refs = 2 * NDOC
        hot = (
            lax.broadcasted_iota(jnp.int32, (512, refs), 0)
            == jnp.broadcast_to(ids[pl.ds(r, 1), :], (512, refs))
        ).astype(jnp.float32)
        hot = hot.astype(jnp.bfloat16)

        def whole(a):
            return a.astype(jnp.float32).astype(jnp.bfloat16)

        blocks = jnp.dot(whole(kept[...]), hot, preferred_element_type=jnp.float32)
        spread = whole(
            (
                lax.broadcasted_iota(jnp.int32, (SLOTS, span), 1) // BLK
                == lax.broadcasted_iota(jnp.int32, (SLOTS, span), 0)
            ).astype(jnp.int32)
        )
        across = (((0,), (0,)), ((), ()))
        block = lax.dot_general(
            blocks.astype(jnp.bfloat16), spread, across, preferred_element_type=jnp.float32
        ).astype(jnp.int32)
        held = jnp.dot(
            whole(jnp.broadcast_to(counts[...], (8, 512))), hot, preferred_element_type=jnp.float32
        )
        eighth = jnp.full((8, span), 0.125, jnp.bfloat16)
        count = lax.dot_general(
            held.astype(jnp.bfloat16), eighth, across, preferred_element_type=jnp.float32
        ).astype(jnp.int32)
        token = lax.broadcasted_iota(jnp.int32, (refs, span), 1)
        ref = lax.broadcasted_iota(jnp.int32, (refs, span), 0)
        position = lax.rem(ref, NDOC) * (DOC_BLKS * BLK) + block * BLK + lax.rem(token, BLK)
        dead = (token // BLK >= count).astype(jnp.int32)
        first = ref < NDOC

        def compare(k, dead):
            row = jnp.where(first, rows[0, k], rows[1, k])
            return dead | (position == row).astype(jnp.int32)

        dead = lax.fori_loop(0, 128, compare, dead)
        shut = jnp.where(dead > 0, -jnp.inf, 0.0)
        for i in range(2):
            for j in range(NDOC):
                bias[i, :, pl.ds(j * span, span)] = shut[i * NDOC + j : i * NDOC + j + 1]
            bias[i, :, pl.ds(NDOC * span, 128)] = jnp.zeros((1, 128), jnp.float32)

    def h_at(row_x, head):
        return hg.at[
            pl.ds(pl.multiple_of(row_x * 256, 256), 256),
            pl.ds(pl.multiple_of(head * 256, 256), 256),
        ]

    hx = []
    for k in range(1, NX):
        cols = pl.ds(pl.multiple_of(at_x(k) * 256, 256), 256)
        hx.append(
            go(send(hid.at[:, cols], h_at(x, h), hx_s.at[k - 1], hx_r.at[k - 1], dev_x(k)))
        )
    own_h = pltpu.make_async_copy(
        hid.at[:, pl.ds(pl.multiple_of(x * 256, 256), 256)], h_at(x, h), own_sem.at[6]
    )
    own_h.start()

    def w_step(n, s):
        pair = []
        for way in range(2):
            if s > 1:
                w_copies[(n, s - 1, way)].wait_recv()
        for way in range(2):
            back = (NZ - (s - 1)) if way == 0 else (s - 1)
            block = at_z(back) * 256
            if s < 4:
                rows = pl.ds(pl.multiple_of(block, 256), 256)
            else:
                rows = pl.ds(pl.multiple_of(block + 128 * way, 128), 128)
            ref = wg.at[n, rows]
            i = (n * 4 + s - 1) * 2 + way
            pair.append(go(send(ref, ref, w_s.at[i], w_r.at[i], dev_z(1 if way == 0 else NZ - 1))))
        w_copies[(n, s, 0)], w_copies[(n, s, 1)] = pair

    w_copies = {}

    lead = (0, 0, 1, 2, 3)

    def w_slot(t):
        for n in range(CHUNKS):
            s = t - lead[n]
            if 1 <= s <= 4:
                if s == 1:
                    own[n + 1].wait()
                    if n == 0:
                        own[0].wait()
                w_step(n, s)

    def w_finish(n):
        for way in range(2):
            w_copies[(n, 4, way)].wait_recv()

    w_slot(1)

    def look_up(d, found):
        return jnp.where(ids[...] == d, place[d], found)

    found = lax.fori_loop(0, 512, look_up, jnp.zeros((32, 32), jnp.int32), unroll=8)
    placed[...] = found
    owner, local = found // 16, lax.rem(found, 16)
    order = lax.broadcasted_iota(jnp.int32, (32, 32), 1)
    line = lax.broadcasted_iota(jnp.int32, (32, 32), 0)
    spare = 32 * 16
    key = jnp.where(owner == r, order * 16 + local, spare)
    first = jnp.min(key, axis=1, keepdims=True)
    second_key = jnp.min(jnp.where(key > first, key, spare), axis=1, keepdims=True)
    choice = jnp.zeros((32, 1), jnp.int32)
    spares = jnp.zeros((32, 1), jnp.int32)
    worst = jnp.zeros((32, 1), jnp.int32)
    above = jnp.zeros((32, 1), jnp.int32)
    below = jnp.zeros((32, 1), jnp.int32)
    target_z = lax.broadcasted_iota(jnp.int32, (32, 1), 0) // NX
    for zo in range(NZ):
        doubled = jnp.zeros((32, 1), jnp.int32)
        pick = jnp.zeros((32, 1), jnp.int32)
        for xo in range(NX):
            held = jnp.sum((owner == zo * NX + xo).astype(jnp.int32), axis=1, keepdims=True)
            twice = (held > 1).astype(jnp.int32)
            doubled = doubled + twice
            pick = jnp.maximum(pick, twice * xo)
        worst = jnp.maximum(worst, doubled)
        away = lax.rem(zo - target_z + NZ, NZ)
        above = above + jnp.where((away >= 1) & (away <= 4), doubled, 0)
        below = below + jnp.where(away >= 5, doubled, 0)
        choice = jnp.where(z == zo, pick, choice)
        spares = jnp.where(z == zo, doubled, spares)
    worst = jnp.maximum(worst, jnp.maximum(above, below))
    worst = jnp.broadcast_to(jnp.max(worst, axis=0, keepdims=True), (32, 1))
    mine_row = placed[pl.ds(r, 1), :] // 16
    mine_wide = jnp.broadcast_to(mine_row, (32, 32))
    mine_col = jnp.sum(jnp.where(order == line, mine_wide, 0), axis=1, keepdims=True)
    later = jnp.max(
        ((mine_wide == mine_col) & (order < line)).astype(jnp.int32), axis=1, keepdims=True
    )
    away = lax.rem(mine_col // NX - z + NZ, NZ)
    spare_slot = jnp.where(away == 0, 32, jnp.where(away <= 4, 33, 34))
    slot = jnp.where(later > 0, spare_slot, mine_col)
    lane = lax.broadcasted_iota(jnp.int32, (32, 128), 1)
    table[...] = jnp.where(
        lane == 0,
        lax.rem(first, 16),
        jnp.where(lane == 1, lax.rem(second_key, 16), jnp.where(lane == 2, choice, jnp.where(lane == 3, slot, jnp.where(lane == 4, worst, spares)))),
    )
    to_scalars = pltpu.make_async_copy(table, tab, own_sem.at[11])
    to_scalars.start()
    to_scalars.wait()
    flag[0, 0] = tab[0, 4]
    for copy in docs_in:
        copy.wait()

    def pack(rank):
        def one(zt, carry):
            for k in range(NX):
                index = tab[zt * NX + at_x(k), rank]
                if k == 0:
                    here = xr1 if rank else xr
                    here[x, zt, 0] = dk[index]
                    here[x, zt, 1] = dv[index]
                else:
                    xs[k - 1, rank, zt, 0] = dk[index]
                    xs[k - 1, rank, zt, 1] = dv[index]
            return carry

        lax.fori_loop(0, NZ, one, 0)

    def send_docs_x(rank):
        there = (xr1 if rank else xr).at[x]
        copies = []
        for k in range(1, NX):
            i = rank * 3 + k - 1
            copies.append(
                go(send(xs.at[k - 1, rank], there, dx_s.at[i], dx_r.at[i], dev_x(k)))
            )
        return copies

    pack(1)
    docs_x1 = send_docs_x(1)
    w_slot(2)
    pack(0)
    docs_x = send_docs_x(0)
    for copy in hx:
        copy.wait_recv()
    own_h.wait()

    def h_cols(head, rows=slice(0, 1024)):
        return hg.at[
            pl.ds(rows.start, rows.stop - rows.start), pl.ds(pl.multiple_of(head * 256, 256), 256)
        ]

    hy, hs = [], []
    for way, k in ((0, 1), (1, 3)):
        hy.append(go(send(h_cols(h), h_cols(h), hy_s.at[way], hy_r.at[way], dev_y(k))))
    hs.append(go(send(h_cols(h), h_cols(h), hs_s.at[0], hs_r.at[0], sibling)))
    w_slot(3)
    mask()
    w_slot(4)
    for copy in hy:
        copy.wait_recv()
    top, bottom = slice(0, 512), slice(512, 1024)
    left, right = head_y(3), head_y(1)
    hy2 = [
        go(send(h_cols(left, top), h_cols(left, top), hy_s.at[2], hy_r.at[2], dev_y(1))),
        go(send(h_cols(right, bottom), h_cols(right, bottom), hy_s.at[3], hy_r.at[3], dev_y(3))),
    ]
    hs.append(go(send(h_cols(left), h_cols(left), hs_s.at[1], hs_r.at[1], sibling)))
    hs.append(go(send(h_cols(right), h_cols(right), hs_s.at[2], hs_r.at[2], sibling)))
    w_slot(5)
    for copy in hy2:
        copy.wait_recv()
    far = head_y(2)
    hs.append(go(send(h_cols(far), h_cols(far), hs_s.at[3], hs_r.at[3], sibling)))
    for copy in hs:
        copy.wait_recv()

    def product(n, k):
        block = lax.rem(x + k, NX)
        rows = pl.ds(pl.multiple_of(block * 256, 256), 256)
        part[n, block] = jnp.dot(hg[rows, :], wg[n], preferred_element_type=jnp.float32)

    r1_copies, r2_copies = {}, {}

    def multiply(n):
        w_finish(n)
        product(n, 2)
        far_x = at_x(2)
        r1_copies[n] = [
            go(
                send(
                    part.at[n, far_x, pl.ds(128 * way, 128)],
                    r1.at[n, way],
                    r1_s.at[n * 2 + way],
                    r1_r.at[n * 2 + way],
                    dev_x(1 if way == 0 else 3),
                )
            )
            for way in range(2)
        ]

        def rest(k, carry):
            product(n, k)
            return carry

        lax.fori_loop(3, 6, rest, 0)

    def second(n):
        for copy in r1_copies[n]:
            copy.wait_recv()
        part[n, at_x(1), pl.ds(0, 128)] = part[n, at_x(1), pl.ds(0, 128)] + r1[n, 0]
        part[n, at_x(3), pl.ds(128, 128)] = part[n, at_x(3), pl.ds(128, 128)] + r1[n, 1]
        r2_copies[n] = [
            go(
                send(
                    part.at[n, at_x(1 if way == 0 else 3)],
                    r2.at[n, way],
                    r2_s.at[n * 2 + way],
                    r2_r.at[n * 2 + way],
                    dev_x(1 if way == 0 else 3),
                )
            )
            for way in range(2)
        ]

    def third(n):
        for copy in r2_copies[n]:
            copy.wait_recv()
        total = (part[n, x] + r2[n, 0] + r2[n, 1]).astype(jnp.bfloat16)
        if n > 0:
            for i in range(2):
                for g in range(2):
                    q_out[pl.ds(i * 1024 + (2 * n - 2 + g) * 128, 128)] = total[
                        i * 128 : (i + 1) * 128, g * HD : (g + 1) * HD
                    ]
        else:
            nk_out[...] = total[:, :HD]
            nv_out[...] = total[:, HD:]

    for copy in docs_x1:
        copy.wait_recv()

    def extra(zt, carry):
        chosen = tab[zt * NX + x, 2]
        ex[zt] = xr1[chosen, zt]
        return carry

    lax.fori_loop(0, NZ, extra, 0)
    own_e = [
        pltpu.make_async_copy(ex.at[z, kv], held.at[32], own_sem.at[8 + 4 * kv])
        for kv, held in ((0, zk), (1, zv))
    ]
    for copy in own_e:
        copy.start()

    spare_copies = {}

    def spare_step(s):
        for way, (step, reach) in enumerate(((NZ - 1, 4), (1, 3))):
            if s > reach:
                continue
            left_to_go = reach + 1 - s
            target = at_z(NZ - left_to_go if way == 0 else left_to_go)
            if s > 1:
                spare_copies[(s - 1, way)].wait_recv()
                mine = tab[target * NX + x, 5] > 0
                ex[target] = jnp.where(mine, ex[target], inbox[way * 3 + s - 2])
            i = way * 4 + s - 1
            if s < reach:
                there = inbox.at[way * 3 + s - 1]
                spare_copies[(s, way)] = go(
                    send(ex.at[target], there, de_s.at[i], de_r.at[i], dev_z(step))
                )
            else:
                for kv, held in ((0, zk), (1, zv)):
                    j = i if kv == 0 else 8 + way
                    spare_copies[("end", way, kv)] = go(
                        send(
                            ex.at[target, kv],
                            held.at[33 + way],
                            de_s.at[j],
                            de_r.at[j],
                            dev_z(step),
                        )
                    )

    spare_step(1)
    w_slot(6)
    spare_step(2)
    multiply(0)
    w_slot(7)
    spare_step(3)
    spare_step(4)
    for copy in docs_x:
        copy.wait_recv()
    docs_z, own_z = ([], []), []
    for kv, held in ((0, zk), (1, zv)):
        for k in (4, 3, 5, 2, 6, 1, 7):
            i = kv * 7 + k - 1
            docs_z[kv].append(
                go(
                    send(
                        xr.at[:, at_z(k), kv],
                        held.at[pl.ds(z * NX, NX)],
                        dz_s.at[i],
                        dz_r.at[i],
                        dev_z(k),
                    )
                )
            )
        own_z.append(
            pltpu.make_async_copy(
                xr.at[:, z, kv], held.at[pl.ds(z * NX, NX)], own_sem.at[7 if kv == 0 else 13]
            )
        )
        own_z[kv].start()

    def arrived(kv):
        own_z[kv].wait()
        own_e[kv].wait()
        for copy in docs_z[kv]:
            copy.wait_recv()
        for way in range(2):
            spare_copies[("end", way, kv)].wait_recv()

    span = SLOTS * BLK
    factor = math.log2(math.e) / math.sqrt(HD)

    def fetch(kv, held, context, fresh):
        arrived(kv)
        for i in range(2):

            def one(j, carry):
                at = pl.ds(pl.multiple_of(j * span, span), span)
                context[i, at] = held[tab[i * NDOC + j, 3]]
                return carry

            lax.fori_loop(0, NDOC, one, 0)
            context[i, pl.ds(NDOC * span, 128)] = fresh[pl.ds(i * 128, 128)]

    def score(i, p):
        step = i * 4 + p
        scores = lax.dot_general(
            q_out[pl.ds(step * 256, 256)],
            keys[i],
            (((1,), (1,)), ((), ())),
            preferred_element_type=jnp.float32,
        )
        scores = scores * factor + bias[i]
        points[step] = scores
        return jnp.max(scores, axis=-1, keepdims=True)

    def spread_out(i, p, peak):
        step = i * 4 + p
        weights = jnp.exp2(points[step] - peak)
        points[step] = weights
        share = 1.0 / jnp.sum(weights, axis=-1, keepdims=True)
        shares[step] = jnp.broadcast_to(share, (256, 128))

    def heads(p):
        peaks = [score(i, p) for i in range(2)]
        for i in range(2):
            spread_out(i, p, peaks[i])

    def gather_values(step, carry):
        i, p = step // 4, lax.rem(step, 4)
        probs = (points[step] * shares[step][:, :1]).astype(jnp.bfloat16)
        result = jnp.dot(probs, values[i], preferred_element_type=jnp.float32).astype(jnp.bfloat16)
        at = pl.ds(pl.multiple_of(i * 128, 128), 128)
        for g in range(2):
            cols = pl.ds(pl.multiple_of(p * 256 + g * HD, HD), HD)
            out[at, cols] = result[g * 128 : (g + 1) * 128]
        return carry

    multiply(1)
    multiply(2)
    second(0)
    multiply(3)
    second(1)
    multiply(4)
    second(2)
    second(3)
    second(4)
    third(0)
    fetch(0, zk, keys, nk_out)
    for n in range(1, CHUNKS):
        third(n)
        heads(n - 1)
    fetch(1, zv, values, nv_out)
    lax.fori_loop(0, 8, gather_values, 0)
    for copy in started:
        copy.wait_send()


def fused(rows, place, ids, kept, counts, hid, dk, dv, wq, wk, wv):
    vmem = pl.BlockSpec(memory_space=pltpu.VMEM)
    smem = pl.BlockSpec(memory_space=pltpu.SMEM)
    anym = pl.BlockSpec(memory_space=pl.ANY)
    dma = pltpu.SemaphoreType.DMA
    bf16, f32 = jnp.bfloat16, jnp.float32
    context = NDOC * SLOTS * BLK + 128
    return pl.pallas_call(
        exchange_kernel,
        out_shape=(
            jax.ShapeDtypeStruct((256, 1024), bf16),
            jax.ShapeDtypeStruct((2048, HD), bf16),
            jax.ShapeDtypeStruct((256, HD), bf16),
            jax.ShapeDtypeStruct((256, HD), bf16),
            jax.ShapeDtypeStruct((1, 1), jnp.int32),
        ),
        in_specs=[smem, smem, vmem, vmem, vmem, anym, anym, anym, anym, anym, anym],
        out_specs=(vmem, vmem, vmem, vmem, smem),
        scratch_shapes=[
            pltpu.VMEM((32, 32), jnp.int32),
            pltpu.VMEM((32, 128), jnp.int32),
            pltpu.SMEM((32, 128), jnp.int32),
            pltpu.VMEM((16, 128, HD), bf16),
            pltpu.VMEM((16, 128, HD), bf16),
            pltpu.VMEM((2, context, HD), bf16),
            pltpu.VMEM((2, context, HD), bf16),
            pltpu.VMEM((2, 1, context), f32),
            pltpu.VMEM((8, 256, context), f32),
            pltpu.VMEM((8, 256, 128), f32),
            pltpu.VMEM((1024, 2048), bf16),
            pltpu.VMEM((CHUNKS, 2048, COLS), bf16),
            pltpu.VMEM((CHUNKS, NX, 256, COLS), f32),
            pltpu.VMEM((CHUNKS, 2, 128, COLS), f32),
            pltpu.VMEM((CHUNKS, 2, 256, COLS), f32),
            pltpu.VMEM((3, 2, NZ, 2, 128, HD), bf16),
            pltpu.VMEM((NX, NZ, 2, 128, HD), bf16),
            pltpu.VMEM((NX, NZ, 2, 128, HD), bf16),
            pltpu.VMEM((NZ, 2, 128, HD), bf16),
            pltpu.VMEM((5, 2, 128, HD), bf16),
            pltpu.VMEM((35, 128, HD), bf16),
            pltpu.VMEM((35, 128, HD), bf16),
            dma((14,)),
            dma((3,)),
            dma((3,)),
            dma((4,)),
            dma((4,)),
            dma((4,)),
            dma((4,)),
            dma((40,)),
            dma((40,)),
            dma((10,)),
            dma((10,)),
            dma((10,)),
            dma((10,)),
            dma((6,)),
            dma((6,)),
            dma((14,)),
            dma((14,)),
            dma((10,)),
            dma((10,)),
        ],
        compiler_params=pltpu.CompilerParams(
            collective_id=0, has_side_effects=True, vmem_limit_bytes=60 * 2**20
        ),
    )(rows, place, ids, kept, counts, hid, dk, dv, wq, wk, wv)


def shards(
    hidden,
    w_query,
    w_key,
    w_value,
    doc_keys,
    doc_values,
    slot_counts,
    kept_blocks,
    doc_ids,
    doc_place,
    recompute_rows,
):
    owners = lax.axis_size("req")
    refs = 2 * NDOC
    ids = doc_ids.reshape(owners, refs)
    attended, queries, keys_new, values_new, flag = fused(
        recompute_rows,
        doc_place,
        ids,
        kept_blocks.reshape(512, SLOTS).T,
        slot_counts.T,
        hidden.reshape(256, -1),
        doc_keys.reshape(16, 128, HD),
        doc_values.reshape(16, 128, HD),
        w_query,
        w_key,
        w_value,
    )

    def again():
        return general(
            queries.reshape(2, 8, 128, HD).transpose(0, 2, 1, 3).reshape(256, 1024),
            keys_new,
            values_new,
            doc_keys,
            doc_values,
            slot_counts,
            kept_blocks,
            doc_ids,
            doc_place,
            recompute_rows,
        ).reshape(256, 1024)

    attended = lax.cond(flag[0, 0] > 1, again, lambda: attended)
    return (
        attended.reshape(2, 128, 1024),
        keys_new.reshape(2, 128, HD),
        values_new.reshape(2, 128, HD),
    )


def solution(mesh):
    return jax.shard_map(
        shards,
        mesh=mesh,
        in_specs=(
            P("req", None, "head"),
            P("req", "head"),
            P("req", "head"),
            P("req", "head"),
            P("req", "head", None, None),
            P("req", "head", None, None),
            P(None, "head"),
            P(None, "head", None),
            P(),
            P(),
            P("req", None),
        ),
        out_specs=(P("req", None, "head"), P("req", None, "head"), P("req", None, "head")),
        check_vma=False,
    )
```

```python
import math

import jax
import jax.numpy as jnp
from jax import lax
from jax.experimental import pallas as pl
from jax.experimental.pallas import tpu as pltpu
from jax.sharding import PartitionSpec as P

QH = 64
KVH = 8
HD = 128
BLK = 16
DOC_BLKS = 16
SLOTS = 8
NDOC = 16


def attend(block_queries, context_keys, context_values, live, scale):
    scores = (
        jnp.einsum("rgd,kd->rgk", block_queries, context_keys, preferred_element_type=jnp.float32)
        * scale
    )
    scores = jnp.where(live[None, None, :], scores, -jnp.inf)
    peak = jnp.max(scores, axis=-1, keepdims=True)
    weights = jnp.exp(scores - peak)
    probs = (weights / jnp.sum(weights, axis=-1, keepdims=True)).astype(jnp.bfloat16)
    result = jnp.einsum("rgk,kd->rgd", probs, context_values, preferred_element_type=jnp.float32)
    return result.astype(jnp.bfloat16).reshape(block_queries.shape[0], -1)


def general(
    queries,
    keys_new,
    values_new,
    doc_keys,
    doc_values,
    slot_counts,
    kept_blocks,
    doc_ids,
    doc_place,
    recompute_rows,
):
    req_here, rows_req, heads_here = 2, queries.shape[0] // 2, 1
    group = QH // KVH
    span = SLOTS * BLK
    scale = 1.0 / math.sqrt(HD)
    owners = lax.axis_size("req")
    mine = lax.axis_index("req")
    docs_here = doc_keys.shape[0]
    refs = req_here * NDOC
    capacity = 2 * (refs // owners)
    placed = doc_place[doc_ids]
    owner_all = (placed // docs_here).reshape(owners, refs)
    local_all = (placed % docs_here).reshape(owners, refs)
    order = jnp.arange(refs, dtype=jnp.int32)
    earlier = (owner_all[:, :, None] == owner_all[:, None, :]) & (
        order[None, None, :] < order[None, :, None]
    )
    rank = jnp.sum(earlier.astype(jnp.int32), axis=2)
    slot_ids = jnp.arange(capacity, dtype=jnp.int32)
    match = (
        (owner_all == mine)[:, :, None] & (rank[:, :, None] == slot_ids[None, None, :])
    ).astype(jnp.int32)
    picked = jnp.sum(match * local_all[:, :, None], axis=1)
    used = jnp.sum(match, axis=1) > 0

    def pack(cache):
        selected = cache[picked]
        return jnp.where(used[:, :, None, None, None], selected, jnp.zeros_like(selected))

    got_keys = lax.all_to_all(pack(doc_keys), "req", split_axis=0, concat_axis=0, tiled=True)
    got_values = lax.all_to_all(pack(doc_values), "req", split_axis=0, concat_axis=0, tiled=True)
    own_owner = lax.dynamic_index_in_dim(owner_all, mine, 0, False)
    own_rank = lax.dynamic_index_in_dim(rank, mine, 0, False)
    where_row = own_owner * capacity + own_rank
    tail = got_keys.shape[2:]
    fetched_keys = got_keys.reshape((owners * capacity,) + tail)[where_row].reshape(
        (req_here, NDOC) + tail
    )
    fetched_values = got_values.reshape((owners * capacity,) + tail)[where_row].reshape(
        (req_here, NDOC) + tail
    )
    queries = queries.reshape(req_here, rows_req, heads_here, group, HD)
    keys_new = keys_new.reshape(req_here, rows_req, heads_here, HD)
    values_new = values_new.reshape(req_here, rows_req, heads_here, HD)
    my_ids = lax.dynamic_slice_in_dim(doc_ids, mine * req_here, req_here, 0)
    offsets = jnp.arange(NDOC, dtype=jnp.int32)[:, None, None] * (DOC_BLKS * BLK)
    inner = jnp.arange(BLK, dtype=jnp.int32)[None, None, :]
    slot_index = jnp.arange(SLOTS, dtype=jnp.int32)[None, :, None]
    block_rows = 128
    request_outputs = []
    for request in range(req_here):
        ids = my_ids[request]
        positions = recompute_rows[request]
        blocks = kept_blocks[ids, 0]
        count_here = slot_counts[ids, 0]
        key_pos = (offsets + blocks[:, :, None] * BLK + inner).reshape(-1)
        valid = (slot_index < count_here[:, None, None]) & (inner >= 0)
        replaced = jnp.any(key_pos[:, None] == positions[None, :], axis=1)
        live = jnp.concatenate(
            [valid.reshape(-1) & jnp.logical_not(replaced), jnp.ones((rows_req,), bool)]
        )
        context_keys = jnp.concatenate(
            [fetched_keys[request, :, 0].reshape(NDOC * span, HD), keys_new[request, :, 0]], axis=0
        )
        context_values = jnp.concatenate(
            [fetched_values[request, :, 0].reshape(NDOC * span, HD), values_new[request, :, 0]],
            axis=0,
        )
        query_blocks = queries[request, :, 0].reshape(rows_req // block_rows, block_rows, group, HD)
        result = lax.map(
            lambda block_queries: attend(block_queries, context_keys, context_values, live, scale),
            query_blocks,
        )
        head_outputs = result.reshape(rows_req, group * HD)
        request_outputs.append(head_outputs)
    return jnp.stack(request_outputs, axis=0)


MESH = pl.DeviceIdType.MESH
NX, NZ, NY = 4, 8, 4
COLS = 256
CHUNKS = 5


def exchange_kernel(
    rows,
    place,
    ids_in,
    kept,
    counts,
    hid,
    dk_in,
    dv_in,
    wq,
    wk,
    wv,
    out,
    q_out,
    nk_out,
    nv_out,
    flag,
    ids,
    placed,
    table,
    tab,
    dk,
    dv,
    keys,
    values,
    bias,
    points,
    shares,
    hg,
    wg,
    part,
    r1,
    r2,
    xs,
    xr,
    xr1,
    ex,
    inbox,
    zk,
    zv,
    own_sem,
    hx_s,
    hx_r,
    hy_s,
    hy_r,
    hs_s,
    hs_r,
    w_s,
    w_r,
    r1_s,
    r1_r,
    r2_s,
    r2_r,
    dx_s,
    dx_r,
    dz_s,
    dz_r,
    de_s,
    de_r,
):
    r = lax.axis_index("req")
    h = lax.axis_index("head")
    z, x = r // NX, lax.rem(r, NX)
    y, c = h // 2, lax.rem(h, 2)

    def at_x(k):
        return lax.rem(x + k, NX)

    def at_z(k):
        return lax.rem(z + k, NZ)

    def dev_x(k):
        return (z * NX + at_x(k), h)

    def dev_z(k):
        return (at_z(k) * NX + x, h)

    def head_y(k):
        return lax.rem(y + k, NY) * 2 + c

    def dev_y(k):
        return (r, head_y(k))

    sibling = (r, y * 2 + 1 - c)

    def send(src, dst, s, d, device):
        return pltpu.make_async_remote_copy(
            src_ref=src, dst_ref=dst, send_sem=s, recv_sem=d, device_id=device, device_id_type=MESH
        )

    docs_in = [
        pltpu.make_async_copy(dk_in, dk, own_sem.at[9]),
        pltpu.make_async_copy(dv_in, dv, own_sem.at[10]),
    ]
    own = []
    own.append(
        pltpu.make_async_copy(wk, wg.at[0, pl.ds(z * 256, 256), pl.ds(0, HD)], own_sem.at[0])
    )
    own.append(
        pltpu.make_async_copy(wv, wg.at[0, pl.ds(z * 256, 256), pl.ds(HD, HD)], own_sem.at[5])
    )
    for n in range(4):
        own.append(
            pltpu.make_async_copy(
                wq.at[:, pl.ds(n * COLS, COLS)],
                wg.at[n + 1, pl.ds(z * 256, 256)],
                own_sem.at[n + 1],
            )
        )
    for copy in own + docs_in:
        copy.start()

    barrier = pltpu.get_barrier_semaphore()
    for k in range(1, NX):
        pl.semaphore_signal(barrier, inc=1, device_id=dev_x(k), device_id_type=MESH)
    for k in range(1, NZ):
        pl.semaphore_signal(barrier, inc=1, device_id=dev_z(k), device_id_type=MESH)
    for k in (1, 3):
        pl.semaphore_signal(barrier, inc=1, device_id=dev_y(k), device_id_type=MESH)
    pl.semaphore_signal(barrier, inc=1, device_id=sibling, device_id_type=MESH)
    pl.semaphore_wait(barrier, 13)

    started = []

    def go(copy):
        copy.start()
        started.append(copy)
        return copy

    def mask():
        span = SLOTS * BLK
        refs = 2 * NDOC
        hot = (
            lax.broadcasted_iota(jnp.int32, (512, refs), 0)
            == jnp.broadcast_to(ids[pl.ds(r, 1), :], (512, refs))
        ).astype(jnp.float32)
        hot = hot.astype(jnp.bfloat16)

        def whole(a):
            return a.astype(jnp.float32).astype(jnp.bfloat16)

        blocks = jnp.dot(whole(kept[...]), hot, preferred_element_type=jnp.float32)
        spread = whole(
            (
                lax.broadcasted_iota(jnp.int32, (SLOTS, span), 1) // BLK
                == lax.broadcasted_iota(jnp.int32, (SLOTS, span), 0)
            ).astype(jnp.int32)
        )
        across = (((0,), (0,)), ((), ()))
        block = lax.dot_general(
            blocks.astype(jnp.bfloat16), spread, across, preferred_element_type=jnp.float32
        ).astype(jnp.int32)
        held = jnp.dot(
            whole(jnp.broadcast_to(counts[...], (8, 512))), hot, preferred_element_type=jnp.float32
        )
        eighth = jnp.full((8, span), 0.125, jnp.bfloat16)
        count = lax.dot_general(
            held.astype(jnp.bfloat16), eighth, across, preferred_element_type=jnp.float32
        ).astype(jnp.int32)
        token = lax.broadcasted_iota(jnp.int32, (refs, span), 1)
        ref = lax.broadcasted_iota(jnp.int32, (refs, span), 0)
        position = lax.rem(ref, NDOC) * (DOC_BLKS * BLK) + block * BLK + lax.rem(token, BLK)
        dead = (token // BLK >= count).astype(jnp.int32)
        first = ref < NDOC

        def compare(k, dead):
            row = jnp.where(first, rows[0, k], rows[1, k])
            return dead | (position == row).astype(jnp.int32)

        dead = lax.fori_loop(0, 128, compare, dead)
        shut = jnp.where(dead > 0, -jnp.inf, 0.0)
        for i in range(2):
            for j in range(NDOC):
                bias[i, :, pl.ds(j * span, span)] = shut[i * NDOC + j : i * NDOC + j + 1]
            bias[i, :, pl.ds(NDOC * span, 128)] = jnp.zeros((1, 128), jnp.float32)

    def h_at(row_x, head):
        return hg.at[
            pl.ds(pl.multiple_of(row_x * 256, 256), 256),
            pl.ds(pl.multiple_of(head * 256, 256), 256),
        ]

    hx = []
    for k in range(1, NX):
        cols = pl.ds(pl.multiple_of(at_x(k) * 256, 256), 256)
        hx.append(
            go(send(hid.at[:, cols], h_at(x, h), hx_s.at[k - 1], hx_r.at[k - 1], dev_x(k)))
        )
    own_h = pltpu.make_async_copy(
        hid.at[:, pl.ds(pl.multiple_of(x * 256, 256), 256)], h_at(x, h), own_sem.at[6]
    )
    own_h.start()

    def w_step(n, s):
        pair = []
        for way in range(2):
            if s > 1:
                w_copies[(n, s - 1, way)].wait_recv()
        for way in range(2):
            back = (NZ - (s - 1)) if way == 0 else (s - 1)
            block = at_z(back) * 256
            if s < 4:
                rows = pl.ds(pl.multiple_of(block, 256), 256)
            else:
                rows = pl.ds(pl.multiple_of(block + 128 * way, 128), 128)
            ref = wg.at[n, rows]
            i = (n * 4 + s - 1) * 2 + way
            pair.append(go(send(ref, ref, w_s.at[i], w_r.at[i], dev_z(1 if way == 0 else NZ - 1))))
        w_copies[(n, s, 0)], w_copies[(n, s, 1)] = pair

    w_copies = {}

    lead = (0, 0, 1, 2, 3)

    def w_slot(t):
        for n in range(CHUNKS):
            s = t - lead[n]
            if 1 <= s <= 4:
                if s == 1:
                    own[n + 1].wait()
                    if n == 0:
                        own[0].wait()
                w_step(n, s)

    def w_finish(n):
        for way in range(2):
            w_copies[(n, 4, way)].wait_recv()

    w_slot(1)

    def whole_bf16(a):
        return a.astype(jnp.float32).astype(jnp.bfloat16)

    column = lax.broadcasted_iota(jnp.int32, (32, 64), 1)
    for i in range(2):
        chosen = whole_bf16(
            (column == 2 * lax.broadcasted_iota(jnp.int32, (32, 64), 0) + i).astype(jnp.int32)
        )
        high, low = (
            lax.dot_general(
                chosen,
                whole_bf16(digits),
                (((1,), (1,)), ((), ())),
                preferred_element_type=jnp.float32,
            )
            for digits in (ids_in[...] // 16, lax.rem(ids_in[...], 16))
        )
        ids[:, i * NDOC : (i + 1) * NDOC] = (high * 16.0 + low).astype(jnp.int32)

    def look_up(d, found):
        return jnp.where(ids[...] == d, place[d], found)

    found = lax.fori_loop(0, 512, look_up, jnp.zeros((32, 32), jnp.int32), unroll=8)
    placed[...] = found
    owner, local = found // 16, lax.rem(found, 16)
    order = lax.broadcasted_iota(jnp.int32, (32, 32), 1)
    line = lax.broadcasted_iota(jnp.int32, (32, 32), 0)
    spare = 32 * 16
    key = jnp.where(owner == r, order * 16 + local, spare)
    first = jnp.min(key, axis=1, keepdims=True)
    second_key = jnp.min(jnp.where(key > first, key, spare), axis=1, keepdims=True)
    choice = jnp.zeros((32, 1), jnp.int32)
    spares = jnp.zeros((32, 1), jnp.int32)
    worst = jnp.zeros((32, 1), jnp.int32)
    above = jnp.zeros((32, 1), jnp.int32)
    below = jnp.zeros((32, 1), jnp.int32)
    target_z = lax.broadcasted_iota(jnp.int32, (32, 1), 0) // NX
    for zo in range(NZ):
        doubled = jnp.zeros((32, 1), jnp.int32)
        pick = jnp.zeros((32, 1), jnp.int32)
        for xo in range(NX):
            held = jnp.sum((owner == zo * NX + xo).astype(jnp.int32), axis=1, keepdims=True)
            twice = (held > 1).astype(jnp.int32)
            doubled = doubled + twice
            pick = jnp.maximum(pick, twice * xo)
        worst = jnp.maximum(worst, doubled)
        away = lax.rem(zo - target_z + NZ, NZ)
        above = above + jnp.where((away >= 1) & (away <= 4), doubled, 0)
        below = below + jnp.where(away >= 5, doubled, 0)
        choice = jnp.where(z == zo, pick, choice)
        spares = jnp.where(z == zo, doubled, spares)
    worst = jnp.maximum(worst, jnp.maximum(above, below))
    worst = jnp.broadcast_to(jnp.max(worst, axis=0, keepdims=True), (32, 1))
    mine_row = placed[pl.ds(r, 1), :] // 16
    mine_wide = jnp.broadcast_to(mine_row, (32, 32))
    mine_col = jnp.sum(jnp.where(order == line, mine_wide, 0), axis=1, keepdims=True)
    later = jnp.max(
        ((mine_wide == mine_col) & (order < line)).astype(jnp.int32), axis=1, keepdims=True
    )
    away = lax.rem(mine_col // NX - z + NZ, NZ)
    spare_slot = jnp.where(away == 0, 32, jnp.where(away <= 4, 33, 34))
    slot = jnp.where(later > 0, spare_slot, mine_col)
    lane = lax.broadcasted_iota(jnp.int32, (32, 128), 1)
    table[...] = jnp.where(
        lane == 0,
        lax.rem(first, 16),
        jnp.where(lane == 1, lax.rem(second_key, 16), jnp.where(lane == 2, choice, jnp.where(lane == 3, slot, jnp.where(lane == 4, worst, spares)))),
    )
    to_scalars = pltpu.make_async_copy(table, tab, own_sem.at[11])
    to_scalars.start()
    to_scalars.wait()
    flag[0, 0] = tab[0, 4]
    for copy in docs_in:
        copy.wait()

    def pack(rank):
        def one(zt, carry):
            for k in range(NX):
                index = tab[zt * NX + at_x(k), rank]
                if k == 0:
                    here = xr1 if rank else xr
                    here[x, zt, 0] = dk[index]
                    here[x, zt, 1] = dv[index]
                else:
                    xs[k - 1, rank, zt, 0] = dk[index]
                    xs[k - 1, rank, zt, 1] = dv[index]
            return carry

        lax.fori_loop(0, NZ, one, 0)

    def send_docs_x(rank, kv=None):
        there = (xr1 if rank else xr).at[x]
        copies = []
        for k in range(1, NX):
            here = xs.at[k - 1, rank]
            i = rank * 6 + k - 1
            if kv is not None:
                i += kv * 3
            src, dst = (here, there) if kv is None else (here.at[:, kv], there.at[:, kv])
            copies.append(go(send(src, dst, dx_s.at[i], dx_r.at[i], dev_x(k))))
        return copies

    pack(1)
    docs_x1 = send_docs_x(1)
    w_slot(2)
    pack(0)
    docs_x = [send_docs_x(0, 0), send_docs_x(0, 1)]
    for copy in hx:
        copy.wait_recv()
    own_h.wait()

    def h_cols(head, rows=slice(0, 1024)):
        return hg.at[
            pl.ds(rows.start, rows.stop - rows.start), pl.ds(pl.multiple_of(head * 256, 256), 256)
        ]

    hy, hs = [], []
    for way, k in ((0, 1), (1, 3)):
        hy.append(go(send(h_cols(h), h_cols(h), hy_s.at[way], hy_r.at[way], dev_y(k))))
    hs.append(go(send(h_cols(h), h_cols(h), hs_s.at[0], hs_r.at[0], sibling)))
    w_slot(3)
    mask()
    w_slot(4)
    for copy in hy:
        copy.wait_recv()
    top, bottom = slice(0, 512), slice(512, 1024)
    left, right = head_y(3), head_y(1)
    hy2 = [
        go(send(h_cols(left, top), h_cols(left, top), hy_s.at[2], hy_r.at[2], dev_y(1))),
        go(send(h_cols(right, bottom), h_cols(right, bottom), hy_s.at[3], hy_r.at[3], dev_y(3))),
    ]
    hs.append(go(send(h_cols(left), h_cols(left), hs_s.at[1], hs_r.at[1], sibling)))
    hs.append(go(send(h_cols(right), h_cols(right), hs_s.at[2], hs_r.at[2], sibling)))
    w_slot(5)
    for copy in hy2:
        copy.wait_recv()
    far = head_y(2)
    hs.append(go(send(h_cols(far), h_cols(far), hs_s.at[3], hs_r.at[3], sibling)))
    for copy in hs:
        copy.wait_recv()

    def product(n, k):
        block = lax.rem(x + k, NX)
        rows = pl.ds(pl.multiple_of(block * 256, 256), 256)
        part[n, block] = jnp.dot(hg[rows, :], wg[n], preferred_element_type=jnp.float32)

    r1_copies, r2_copies = {}, {}

    def multiply(n):
        w_finish(n)
        product(n, 2)
        far_x = at_x(2)
        r1_copies[n] = [
            go(
                send(
                    part.at[n, far_x, pl.ds(128 * way, 128)],
                    r1.at[n, way],
                    r1_s.at[n * 2 + way],
                    r1_r.at[n * 2 + way],
                    dev_x(1 if way == 0 else 3),
                )
            )
            for way in range(2)
        ]

        def rest(k, carry):
            product(n, k)
            return carry

        lax.fori_loop(3, 6, rest, 0)

    def second(n):
        for copy in r1_copies[n]:
            copy.wait_recv()
        part[n, at_x(1), pl.ds(0, 128)] = part[n, at_x(1), pl.ds(0, 128)] + r1[n, 0]
        part[n, at_x(3), pl.ds(128, 128)] = part[n, at_x(3), pl.ds(128, 128)] + r1[n, 1]
        r2_copies[n] = [
            go(
                send(
                    part.at[n, at_x(1 if way == 0 else 3)],
                    r2.at[n, way],
                    r2_s.at[n * 2 + way],
                    r2_r.at[n * 2 + way],
                    dev_x(1 if way == 0 else 3),
                )
            )
            for way in range(2)
        ]

    def third(n):
        for copy in r2_copies[n]:
            copy.wait_recv()
        total = (part[n, x] + r2[n, 0] + r2[n, 1]).astype(jnp.bfloat16)
        if n > 0:
            for i in range(2):
                for g in range(2):
                    q_out[pl.ds(i * 1024 + (2 * n - 2 + g) * 128, 128)] = total[
                        i * 128 : (i + 1) * 128, g * HD : (g + 1) * HD
                    ]
        else:
            nk_out[...] = total[:, :HD]
            nv_out[...] = total[:, HD:]

    for copy in docs_x1:
        copy.wait_recv()

    def extra(zt, carry):
        chosen = tab[zt * NX + x, 2]
        ex[zt] = xr1[chosen, zt]
        return carry

    lax.fori_loop(0, NZ, extra, 0)
    own_e = [
        pltpu.make_async_copy(ex.at[z, kv], held.at[32], own_sem.at[8 + 4 * kv])
        for kv, held in ((0, zk), (1, zv))
    ]
    for copy in own_e:
        copy.start()

    spare_copies = {}

    def spare_step(s):
        for way, (step, reach) in enumerate(((NZ - 1, 4), (1, 3))):
            if s > reach:
                continue
            left_to_go = reach + 1 - s
            target = at_z(NZ - left_to_go if way == 0 else left_to_go)
            if s > 1:
                spare_copies[(s - 1, way)].wait_recv()
                mine = tab[target * NX + x, 5] > 0
                ex[target] = jnp.where(mine, ex[target], inbox[way * 3 + s - 2])
            i = way * 4 + s - 1
            if s < reach:
                there = inbox.at[way * 3 + s - 1]
                spare_copies[(s, way)] = go(
                    send(ex.at[target], there, de_s.at[i], de_r.at[i], dev_z(step))
                )
            else:
                for kv, held in ((0, zk), (1, zv)):
                    j = i if kv == 0 else 8 + way
                    spare_copies[("end", way, kv)] = go(
                        send(
                            ex.at[target, kv],
                            held.at[33 + way],
                            de_s.at[j],
                            de_r.at[j],
                            dev_z(step),
                        )
                    )

    spare_step(1)
    w_slot(6)
    spare_step(2)
    multiply(0)
    w_slot(7)
    spare_step(3)
    spare_step(4)
    docs_z, own_z = ([], []), []
    for kv, held in ((0, zk), (1, zv)):
        for copy in docs_x[kv]:
            copy.wait_recv()
        for k in (4, 3, 5, 2, 6, 1, 7):
            i = kv * 7 + k - 1
            docs_z[kv].append(
                go(
                    send(
                        xr.at[:, at_z(k), kv],
                        held.at[pl.ds(z * NX, NX)],
                        dz_s.at[i],
                        dz_r.at[i],
                        dev_z(k),
                    )
                )
            )
        own_z.append(
            pltpu.make_async_copy(
                xr.at[:, z, kv], held.at[pl.ds(z * NX, NX)], own_sem.at[7 if kv == 0 else 13]
            )
        )
        own_z[kv].start()

    def arrived(kv):
        own_z[kv].wait()
        own_e[kv].wait()
        for copy in docs_z[kv]:
            copy.wait_recv()
        for way in range(2):
            spare_copies[("end", way, kv)].wait_recv()

    span = SLOTS * BLK
    factor = math.log2(math.e) / math.sqrt(HD)

    def fetch(kv, held, context, fresh):
        arrived(kv)
        for i in range(2):

            def one(j, carry):
                at = pl.ds(pl.multiple_of(j * span, span), span)
                context[i, at] = held[tab[i * NDOC + j, 3]]
                return carry

            lax.fori_loop(0, NDOC, one, 0)
            context[i, pl.ds(NDOC * span, 128)] = fresh[pl.ds(i * 128, 128)]

    def score(i, p):
        step = i * 4 + p
        scores = lax.dot_general(
            q_out[pl.ds(step * 256, 256)],
            keys[i],
            (((1,), (1,)), ((), ())),
            preferred_element_type=jnp.float32,
        )
        scores = scores * factor + bias[i]
        points[step] = scores
        return jnp.max(scores, axis=-1, keepdims=True)

    def spread_out(i, p, peak):
        step = i * 4 + p
        weights = jnp.exp2(points[step] - peak)
        points[step] = weights
        share = 1.0 / jnp.sum(weights, axis=-1, keepdims=True)
        shares[step] = jnp.broadcast_to(share, (256, 128))

    def heads(p):
        peaks = [score(i, p) for i in range(2)]
        for i in range(2):
            spread_out(i, p, peaks[i])

    def gather_values(step, carry):
        i, p = step // 4, lax.rem(step, 4)
        probs = (points[step] * shares[step][:, :1]).astype(jnp.bfloat16)
        result = jnp.dot(probs, values[i], preferred_element_type=jnp.float32).astype(jnp.bfloat16)
        at = pl.ds(pl.multiple_of(i * 128, 128), 128)
        for g in range(2):
            cols = pl.ds(pl.multiple_of(p * 256 + g * HD, HD), HD)
            out[at, cols] = result[g * 128 : (g + 1) * 128]
        return carry

    multiply(1)
    multiply(2)
    second(0)
    multiply(3)
    second(1)
    multiply(4)
    second(2)
    second(3)
    second(4)
    third(0)
    fetch(0, zk, keys, nk_out)
    for n in range(1, CHUNKS):
        third(n)
        heads(n - 1)
    fetch(1, zv, values, nv_out)
    lax.fori_loop(0, 8, gather_values, 0, unroll=2)
    for copy in started:
        copy.wait_send()


def fused(rows, place, ids, kept, counts, hid, dk, dv, wq, wk, wv):
    vmem = pl.BlockSpec(memory_space=pltpu.VMEM)
    smem = pl.BlockSpec(memory_space=pltpu.SMEM)
    anym = pl.BlockSpec(memory_space=pl.ANY)
    dma = pltpu.SemaphoreType.DMA
    bf16, f32 = jnp.bfloat16, jnp.float32
    context = NDOC * SLOTS * BLK + 128
    return pl.pallas_call(
        exchange_kernel,
        out_shape=(
            jax.ShapeDtypeStruct((256, 1024), bf16),
            jax.ShapeDtypeStruct((2048, HD), bf16),
            jax.ShapeDtypeStruct((256, HD), bf16),
            jax.ShapeDtypeStruct((256, HD), bf16),
            jax.ShapeDtypeStruct((1, 1), jnp.int32),
        ),
        in_specs=[smem, smem, vmem, vmem, vmem, anym, anym, anym, anym, anym, anym],
        out_specs=(vmem, vmem, vmem, vmem, smem),
        scratch_shapes=[
            pltpu.VMEM((32, 32), jnp.int32),
            pltpu.VMEM((32, 32), jnp.int32),
            pltpu.VMEM((32, 128), jnp.int32),
            pltpu.SMEM((32, 128), jnp.int32),
            pltpu.VMEM((16, 128, HD), bf16),
            pltpu.VMEM((16, 128, HD), bf16),
            pltpu.VMEM((2, context, HD), bf16),
            pltpu.VMEM((2, context, HD), bf16),
            pltpu.VMEM((2, 1, context), f32),
            pltpu.VMEM((8, 256, context), f32),
            pltpu.VMEM((8, 256, 128), f32),
            pltpu.VMEM((1024, 2048), bf16),
            pltpu.VMEM((CHUNKS, 2048, COLS), bf16),
            pltpu.VMEM((CHUNKS, NX, 256, COLS), f32),
            pltpu.VMEM((CHUNKS, 2, 128, COLS), f32),
            pltpu.VMEM((CHUNKS, 2, 256, COLS), f32),
            pltpu.VMEM((3, 2, NZ, 2, 128, HD), bf16),
            pltpu.VMEM((NX, NZ, 2, 128, HD), bf16),
            pltpu.VMEM((NX, NZ, 2, 128, HD), bf16),
            pltpu.VMEM((NZ, 2, 128, HD), bf16),
            pltpu.VMEM((5, 2, 128, HD), bf16),
            pltpu.VMEM((35, 128, HD), bf16),
            pltpu.VMEM((35, 128, HD), bf16),
            dma((14,)),
            dma((3,)),
            dma((3,)),
            dma((4,)),
            dma((4,)),
            dma((4,)),
            dma((4,)),
            dma((40,)),
            dma((40,)),
            dma((10,)),
            dma((10,)),
            dma((10,)),
            dma((10,)),
            dma((9,)),
            dma((9,)),
            dma((14,)),
            dma((14,)),
            dma((10,)),
            dma((10,)),
        ],
        compiler_params=pltpu.CompilerParams(
            collective_id=0, has_side_effects=True, vmem_limit_bytes=60 * 2**20
        ),
    )(rows, place, ids, kept, counts, hid, dk, dv, wq, wk, wv)


def shards(
    hidden,
    w_query,
    w_key,
    w_value,
    doc_keys,
    doc_values,
    slot_counts,
    kept_blocks,
    doc_ids,
    doc_place,
    recompute_rows,
):
    attended, queries, keys_new, values_new, flag = fused(
        recompute_rows,
        doc_place,
        doc_ids.T,
        kept_blocks.reshape(512, SLOTS).T,
        slot_counts.T,
        hidden.reshape(256, -1),
        doc_keys.reshape(16, 128, HD),
        doc_values.reshape(16, 128, HD),
        w_query,
        w_key,
        w_value,
    )

    def again():
        return general(
            queries.reshape(2, 8, 128, HD).transpose(0, 2, 1, 3).reshape(256, 1024),
            keys_new,
            values_new,
            doc_keys,
            doc_values,
            slot_counts,
            kept_blocks,
            doc_ids,
            doc_place,
            recompute_rows,
        ).reshape(256, 1024)

    attended = lax.cond(flag[0, 0] > 1, again, lambda: attended)
    return (
        attended.reshape(2, 128, 1024),
        keys_new.reshape(2, 128, HD),
        values_new.reshape(2, 128, HD),
    )


def solution(mesh):
    return jax.shard_map(
        shards,
        mesh=mesh,
        in_specs=(
            P("req", None, "head"),
            P("req", "head"),
            P("req", "head"),
            P("req", "head"),
            P("req", "head", None, None),
            P("req", "head", None, None),
            P(None, "head"),
            P(None, "head", None),
            P(),
            P(),
            P("req", None),
        ),
        out_specs=(P("req", None, "head"), P("req", None, "head"), P("req", None, "head")),
        check_vma=False,
    )
```
